512 devices in a mesh: bld: 128 (over z, y, core), real: 4 (over x).
Axes of the slice: x: 4, y: 8, z: 8, core: 2. Of those that a mesh axis runs over, the one named last changes fastest.
Arguments:
- site_ln: float32 [64, 16384], P('real', 'bld'), may hold values from -4 to 4
- site_of: int32 [16384], P('bld'), may hold values from 0 to 16383
- county_of: int32 [16384], P('bld'), may hold values from 0 to 15
- tract_of: int32 [16384], P('bld'), may hold values from 0 to 2047
- comp_type: int32 [24, 16384], P(None, 'bld'), may hold values from 0 to 255
- comp_qty: int32 [24, 16384], P(None, 'bld'), may hold values from 0 to 12, as said below
- amplify: float32 [24, 16384], P(None, 'bld'), may hold values from -1.5 to 1.5
- frag_median: float32 [256], replicated, may hold values from -1 to 1
- frag_step: float32 [256], replicated, may hold values from 0.3 to 1
- frag_beta: float32 [256], replicated, may hold values from 0.4 to 0.8
- state_cost: float32 [3, 256], replicated, may hold values from 0.0005 to 0.008
Outputs:
- tract_loss: float32 [2048, 64], P('bld', 'real')
- tract_avg: float32 [2048], P('bld')
The draws below stay inside these ranges and needn't reach their ends.
Inputs may be any that keep to these rules, and one draw needn't show every extreme that they name: `comp_qty`: the quantities tend to grow with the building's index.
All inputs are finite; a program needn't handle non-finite values.
Results may differ from the reference program's by a relative error of at most 0.00036.
Values may be sent and summed in bfloat16 or wider, within the bound.
A program may use at most 64 MiB of HBM per device.

```python
import math
import jax
import jax.numpy as jnp
from jax import lax

GROUPS = 24
TYPES = 256
STATES = 3
COUNTIES = 16
BUILDINGS = 16384
REALS = 64
SITES = 16384
TRACTS = 2048
KEYS = 4096


def draw_comp_qty(key, part):
    position = jnp.arange(BUILDINGS, dtype=jnp.int32)
    ceiling = 4 + 9 * position // BUILDINGS
    values = jax.random.randint(key, (GROUPS, BUILDINGS), 0, ceiling[None, :] + 1)
    values = values.at[0, BUILDINGS - 1].set(12)
    values = values.at[0, 0].set(0)
    return values.astype(jnp.int32)


def building_places(key):
    base = jax.random.fold_in(key, 7001)
    key_site, key_moved, key_county, key_tract, key_high, key_offset = jax.random.split(base, 6)
    site = jax.random.randint(key_site, (BUILDINGS,), 0, SITES)
    moved = jax.random.randint(key_moved, (2, BUILDINGS), 0, 8) == 0
    county = jnp.where(moved[0], jax.random.randint(key_county, (BUILDINGS,), 0, COUNTIES), site * COUNTIES // SITES)
    tract = jnp.where(moved[1], jax.random.randint(key_tract, (BUILDINGS,), 0, TRACTS), site * TRACTS // SITES)
    high_at = jax.random.randint(key_high, (), 0, BUILDINGS)
    low_at = (high_at + 1 + jax.random.randint(key_offset, (), 0, BUILDINGS - 1)) % BUILDINGS
    site = site.at[high_at].set(SITES - 1).at[low_at].set(0)
    county = county.at[high_at].set(COUNTIES - 1).at[low_at].set(0)
    tract = tract.at[high_at].set(TRACTS - 1).at[low_at].set(0)
    return (site.astype(jnp.int32), county.astype(jnp.int32), tract.astype(jnp.int32))


def draw_site_of(key, part):
    return building_places(key)[0]


def draw_county_of(key, part):
    return building_places(key)[1]


def draw_tract_of(key, part):
    return building_places(key)[2]


def draw_site_ln(key, part):
    base = jax.random.fold_in(key, 7002)
    key_level, key_event, key_noise = jax.random.split(base, 3)
    site_county = jnp.arange(SITES, dtype=jnp.int32) * COUNTIES // SITES
    level = jax.random.uniform(key_level, (COUNTIES,), jnp.float32, -0.6, 0.6)
    event = 0.5 * jax.random.normal(key_event, (REALS, COUNTIES), jnp.float32)
    noise = 0.7 * jax.random.normal(key_noise, (REALS, SITES), jnp.float32)
    values = jnp.take(level, site_county)[None, :] + jnp.take(event, site_county, axis=1) + noise
    return jnp.clip(values, -4.0, 4.0).astype(jnp.float32)


def place_ends(array, own_key, smallest, top_value):
    longest = array.shape.index(max(array.shape))
    spots = []
    for shift in (0, 1):
        where = [jax.random.randint(jax.random.fold_in(own_key, axis), (), 0, length) for axis, length in enumerate(array.shape)]
        where[longest] = (where[longest] + shift) % array.shape[longest]
        spots.append(tuple(where))
    return array.at[spots[0]].set(smallest).at[spots[1]].set(top_value)


def levels(own_key, dims, cuts, low, high):
    factor_of = 1.0
    for dim, shards_of in cuts:
        steps = jax.random.uniform(jax.random.fold_in(jax.random.fold_in(own_key, 6), dim), (shards_of,), jnp.float32, low / len(cuts), high / len(cuts))
        factor_of = factor_of * jnp.repeat(jnp.exp(steps), dims[dim] // shards_of).reshape((-1,) + (1,) * (len(dims) - 1 - dim))
    return factor_of


def centred(stream_key, dims, width, limit, cuts=(), held_as=jnp.bfloat16):
    array = width * jax.random.normal(stream_key, dims, jnp.float32)
    if cuts:
        array = array * levels(stream_key, dims, cuts, -0.22, 0.18)
    return jnp.clip(array, -limit, limit).astype(held_as)


def setup_inputs(seed: int = 0) -> dict:
    arg_keys = jax.random.split(jax.random.key(seed), 12)
    site_ln = draw_site_ln(jax.random.fold_in(arg_keys[11], 71), 0)
    site_of = draw_site_of(jax.random.fold_in(arg_keys[11], 71), 0)
    county_of = draw_county_of(jax.random.fold_in(arg_keys[11], 71), 0)
    tract_of = draw_tract_of(jax.random.fold_in(arg_keys[11], 71), 0)
    comp_type = place_ends(jax.random.randint(arg_keys[4], (GROUPS, BUILDINGS), 0, TYPES), jax.random.fold_in(arg_keys[4], 1), 0, TYPES - 1).astype(jnp.int32)
    comp_qty = draw_comp_qty(jax.random.fold_in(arg_keys[11], 71), 0)
    amplify = centred(arg_keys[6], (GROUPS, BUILDINGS), 0.3, 1.5, ((1, 128),), jnp.float32)
    frag_median = jnp.clip(jax.random.uniform(arg_keys[7], (TYPES,), jnp.float32, -1.0, 1.0), -1.0, 1.0)
    frag_step = jnp.clip(jnp.exp(jax.random.uniform(arg_keys[8], (TYPES,), jnp.float32, math.log(0.3), math.log(1.0))), 0.3, 1.0)
    frag_beta = jnp.clip(jax.random.uniform(arg_keys[9], (TYPES,), jnp.float32, 0.4, 0.8), 0.4, 0.8)
    state_cost = jnp.clip(jnp.exp(jax.random.uniform(arg_keys[10], (STATES, TYPES), jnp.float32, math.log(0.0005), math.log(0.008))), 0.0005, 0.008)
    return dict(site_ln=site_ln, site_of=site_of, county_of=county_of, tract_of=tract_of, comp_type=comp_type, comp_qty=comp_qty, amplify=amplify, frag_median=frag_median, frag_step=frag_step, frag_beta=frag_beta, state_cost=state_cost)


surge_peak = 1.0
root_half = 0.7071067811865476


def normal_cdf(value):
    return 0.5 * (1.0 + lax.erf(value * root_half))


def group_damage(log_intensity, amplify_row, type_ids, frag_median, frag_step, frag_beta, state_cost):
    medians = jnp.take(frag_median, type_ids)
    spacing = jnp.take(frag_step, type_ids)
    spread = jnp.take(frag_beta, type_ids)
    demand = log_intensity + amplify_row[None, :]
    expect = jnp.zeros_like(demand)
    cost_prev = jnp.zeros_like(medians)
    damaged_p = demand
    for damage_lvl in range(STATES):
        chance = normal_cdf((demand - medians[None, :] - damage_lvl * spacing[None, :]) / spread[None, :])
        cost_now = jnp.take(state_cost[damage_lvl], type_ids)
        expect = expect + chance * (cost_now - cost_prev)[None, :]
        cost_prev = cost_now
        if damage_lvl == 0:
            damaged_p = chance
    return damaged_p, expect


def reference(site_ln, site_of, county_of, tract_of, comp_type, comp_qty, amplify, frag_median, frag_step, frag_beta, state_cost):
    log_intensity = jnp.take(site_ln, site_of, axis=1)
    key_ids = (county_of[None, :] * TYPES + comp_type).astype(jnp.int32)
    quantity = comp_qty.astype(jnp.float32)
    half_point = float(4 * BUILDINGS * GROUPS // KEYS + 1)

    def collect(running, group_at):
        damaged_p, expect = group_damage(log_intensity, amplify[group_at], comp_type[group_at], frag_median, frag_step, frag_beta, state_cost)
        damaged = (quantity[group_at][None, :] * damaged_p).astype(jnp.bfloat16)
        running = running + jax.ops.segment_sum(damaged.astype(jnp.float32).T, key_ids[group_at], num_segments=KEYS)
        return running, None

    county, _ = lax.scan(collect, jnp.zeros((KEYS, REALS), jnp.float32), jnp.arange(GROUPS))
    surge_cost = (1.0 + surge_peak * county / (county + half_point)).astype(jnp.bfloat16)

    def apply_surge(running, group_at):
        damaged_p, expect = group_damage(log_intensity, amplify[group_at], comp_type[group_at], frag_median, frag_step, frag_beta, state_cost)
        lookup = jnp.take(surge_cost, key_ids[group_at], axis=0).astype(jnp.float32)
        running = running + quantity[group_at][:, None] * expect.T * lookup
        return running, None

    bld_loss, _ = lax.scan(apply_surge, jnp.zeros((BUILDINGS, REALS), jnp.float32), jnp.arange(GROUPS))
    tract_loss = jax.ops.segment_sum(bld_loss, tract_of, num_segments=TRACTS)
    tract_avg = jnp.sum(tract_loss, axis=1) / REALS
    return (tract_loss, tract_avg)
```

```python
import jax
import jax.numpy as jnp
from jax import lax
from jax.experimental import pallas as pl
from jax.experimental.pallas import tpu as pltpu
from jax.sharding import PartitionSpec as P

LINE = 8
GROUPS = 24
TYPES = 256
COUNTIES = 16
LANES = 128
HALF = 8
WIDE = 2 * LANES
REALS_ALL = 64.0
HALF_POINT = 385.0
ROOT_HALF = 0.7071067811865476
MESH = pl.DeviceIdType.MESH
F32 = jnp.float32
BF16 = jnp.bfloat16
HIGHEST = lax.Precision.HIGHEST
NT = (((1,), (1,)), ((), ()))


def lanes_of(table, index):
    return jnp.take_along_axis(table, index, axis=1, mode="promise_in_bounds")


def drain(ref, sem):
    pltpu.make_async_copy(ref, ref, sem).wait()


def kernel(
    site_ln, site_of, county_of, tract_of, comp_type, comp_qty, amplify,
    frag_median, frag_step, frag_beta, state_cost,
    loss_out, avg_out,
    b_site, b_county, b_tract, b_type, b_qty, b_amp,
    t_med, t_step, t_beta, t_cost,
    sites, p_base, p_inv, p_step, p_half, p_c0, p_c1, p_c2,
    hot, spread, args, weight,
    part, got3, half_sum, got4, surge_own, surge,
    dest, terms, tract_part, got6, rows, got7, row, got8,
    loc_sem, par_sem, bld_send, bld_recv,
    s1, r1, s2, r2, s3, r3, s4, r4, s5, r5, s6, r6, s7, r7, s8, r8,
):
    me = lax.axis_index("bld")
    x = lax.axis_index("real")
    z = me // (2 * LINE)
    y = lax.rem(me // 2, LINE)
    c = lax.rem(me, 2)

    def at(zz, yy, cc):
        return {"bld": (zz * LINE + yy) * 2 + cc}

    def send(src, dst, ssem, rsem, who):
        pltpu.make_async_remote_copy(
            src_ref=src, dst_ref=dst, send_sem=ssem, recv_sem=rsem,
            device_id=who, device_id_type=MESH,
        ).start()

    barrier = pltpu.get_barrier_semaphore()

    def hello(who):
        pl.semaphore_signal(barrier, inc=1, device_id=who, device_id_type=MESH)

    hello(at(z, y, 1 - c))
    for i in range(1, LINE):
        for h in range(2):
            hello(at(z, lax.rem(y + i, LINE), h))
            hello(at(lax.rem(z + i, LINE), y, h))
    for i in range(1, 4):
        hello({"real": lax.rem(x + i, 4)})

    buildings = (
        (site_of, b_site), (county_of, b_county), (tract_of, b_tract),
        (comp_type, b_type), (comp_qty, b_qty), (amplify, b_amp),
    )
    tables = ((frag_median, t_med), (frag_step, t_step), (frag_beta, t_beta), (state_cost, t_cost))
    own = [pltpu.make_async_copy(a, b.at[0], loc_sem.at[n]) for n, (a, b) in enumerate(buildings)]
    own += [pltpu.make_async_copy(a, b, par_sem.at[n]) for n, (a, b) in enumerate(tables)]
    for copy in own:
        copy.start()

    pl.semaphore_wait(barrier, 1 + 4 * (LINE - 1) + 3)

    p = y * (1 - c) + z * c
    q = z * (1 - c) + y * c
    mine = sites.at[c, q, p]
    local = pltpu.make_async_copy(site_ln.at[pl.ds(pl.multiple_of(c * HALF, HALF), HALF)], mine, r1.at[c])
    local.start()
    send(site_ln.at[pl.ds(pl.multiple_of((1 - c) * HALF, HALF), HALF)], mine, s1, r1.at[c], at(z, y, 1 - c))
    for i in range(1, LINE):
        pp = lax.rem(p + i, LINE)
        for h in range(2):
            zz = q * (1 - c) + pp * c
            yy = pp * (1 - c) + q * c
            send(site_ln.at[pl.ds(h * HALF, HALF)], mine, s1, r1.at[c], at(zz, yy, h))
    trade = [
        pltpu.make_async_remote_copy(
            src_ref=a, dst_ref=b.at[1], send_sem=bld_send.at[n], recv_sem=bld_recv.at[n],
            device_id=at(z, y, 1 - c), device_id_type=MESH,
        )
        for n, (a, b) in enumerate(buildings)
    ]
    for copy in trade:
        copy.start()

    drain(sites.at[0, z], r1.at[0])
    for i in range(1, LINE):
        send(sites.at[0, z], sites.at[0, z], s2, r2.at[0, i], at(lax.rem(z + i, LINE), y, c))
    drain(sites.at[1, y], r1.at[1])
    for i in range(1, LINE):
        send(sites.at[1, y], sites.at[1, y], s2, r2.at[1, i], at(z, lax.rem(y + i, LINE), c))

    for copy in own:
        copy.wait()
    for copy in trade:
        copy.wait()
    inv_row = ROOT_HALF / t_beta[...]
    step_row = t_step[...] * inv_row
    med_row = t_med[...]
    cost = t_cost[...]

    def cost_rows(level):
        now = cost[level : level + 1]
        if level:
            now = now - cost[level - 1 : level]
        return now[:, :LANES], now[:, LANES:]

    def pair(table):
        return table[0:1], table[1:2]

    looked = (
        (pair(med_row), p_base), (pair(inv_row), p_inv), (pair(step_row), p_step),
        (cost_rows(0), p_c0), (cost_rows(1), p_c1), (cost_rows(2), p_c2),
    )
    for bh in range(2):
        for g in range(0, GROUPS, 8):
            index = b_type[bh, g : g + 8, :]
            low = index & (LANES - 1)
            high = index >= LANES
            for (first, second), into in looked:
                value = jnp.where(
                    high,
                    lanes_of(jnp.broadcast_to(second, (8, LANES)), low),
                    lanes_of(jnp.broadcast_to(first, (8, LANES)), low),
                )
                if into is p_base:
                    value = b_amp[bh, g : g + 8, :] - value
                into[bh, g : g + 8, :] = value
            p_half[bh, g : g + 8, :] = 0.5 * b_qty[bh, g : g + 8, :].astype(F32)

    one = jnp.ones((16, LANES), BF16)
    zero = jnp.zeros((16, LANES), BF16)
    count = lax.broadcasted_iota(jnp.int32, (16, LANES), 0)

    counts = [(count + 16 * n).astype(F32).astype(BF16) for n in range(TYPES // 16)]

    def make_hot(g, _):
        for bh in range(2):
            types = jnp.broadcast_to(b_type[bh, pl.ds(g, 1), :], (16, LANES)).astype(F32).astype(BF16)
            columns = pl.ds(pl.multiple_of(g * WIDE + bh * LANES, LANES), LANES)
            for n in range(TYPES // 16):
                hot[n * 16 : (n + 1) * 16, columns] = jnp.where(types == counts[n], one, zero)
        return 0

    lax.fori_loop(0, GROUPS, make_hot, 0)

    for bh in range(2):
        owner = b_tract[bh] // 16
        place = (owner & 15) * LINE + owner // 16
        place = jnp.broadcast_to(place, (16, LANES)).astype(F32).astype(BF16)
        for n in range(8):
            value = jnp.where(place == counts[n], one, zero)
            for piece in range(3):
                dest[n * 16 : (n + 1) * 16, piece * WIDE + bh * LANES : piece * WIDE + (bh + 1) * LANES] = value

    upper = (count >= HALF).astype(jnp.int32)

    def pair_masks(ref, bh):
        value = jnp.broadcast_to(ref, (16, LANES)) - upper
        value = value.astype(F32).astype(BF16)
        return [jnp.where(value == jnp.asarray(2 * n, BF16), one, zero) for n in range(8)]

    low = [jnp.broadcast_to(b_site[bh] & (LANES - 1), (HALF, LANES)) for bh in range(2)]
    high = [jnp.broadcast_to(b_site[bh] // LANES, (HALF, LANES)) for bh in range(2)]
    level = [jnp.zeros((HALF, LANES), F32) for _ in range(2)]

    def pick(level, route, line):
        for n in range(LINE):
            tile = sites[route, line, n]
            block = (line * 16 + 2 * n) if route == 0 else (n * 16 + line * 2 + 1)
            level = [jnp.where(high[bh] == block, lanes_of(tile, low[bh]), level[bh]) for bh in range(2)]
        return level

    level = pick(level, 0, z)
    level = pick(level, 1, y)
    for i in (1, 7, 2, 6, 3, 5, 4):
        zz = lax.rem(z + LINE - i, LINE)
        drain(sites.at[0, zz], r2.at[0, i])
        level = pick(level, 0, zz)
        yy = lax.rem(y + LINE - i, LINE)
        drain(sites.at[1, yy], r2.at[1, i])
        level = pick(level, 1, yy)

    for bh in range(2):
        masks = pair_masks(b_county[bh], bh)

        def damage(g, _):
            row_at = pl.ds(g, 1)
            arg = (level[bh] + p_base[bh, row_at, :]) * p_inv[bh, row_at, :]
            dam = p_half[bh, row_at, :] * (1.0 + lax.erf(arg))
            args[g * 2 + bh] = arg
            weight[g * 2 + bh] = dam * p_c0[bh, row_at, :]
            twice = jnp.concatenate([dam, dam], axis=0).astype(BF16)
            columns = pl.ds(pl.multiple_of(g * WIDE + bh * LANES, LANES), LANES)
            for n in range(8):
                spread[n * 16 : (n + 1) * 16, columns] = twice * masks[n]
            return 0

        lax.fori_loop(0, GROUPS, damage, 0, unroll=4)

    sums = lax.dot_general(spread[...], hot[...], NT, preferred_element_type=F32)
    part[0] = sums[:, :LANES].reshape(COUNTIES, HALF, LANES)
    part[1] = sums[:, LANES:].reshape(COUNTIES, HALF, LANES)

    for i in range(1, LINE):
        yy = lax.rem(y + i, LINE)
        send(part.at[0, pl.ds(2 * yy, 2)], got3.at[0, y], s3, r3, at(z, yy, c))
        zz = lax.rem(z + i, LINE)
        send(part.at[1, pl.ds(2 * zz, 2)], got3.at[1, z], s3, r3, at(zz, y, c))
    got3[0, y] = part[0, pl.ds(2 * y, 2)]
    got3[1, z] = part[1, pl.ds(2 * z, 2)]

    def more(first, last):
        def weigh(g, _):
            row_at = pl.ds(g, 1)
            for bh in range(2):
                arg = args[g * 2 + bh]
                step = p_step[bh, row_at, :]
                rest = (1.0 + lax.erf(arg - step)) * p_c1[bh, row_at, :]
                rest = rest + (1.0 + lax.erf(arg - 2.0 * step)) * p_c2[bh, row_at, :]
                weight[g * 2 + bh] = weight[g * 2 + bh] + p_half[bh, row_at, :] * rest
            return 0

        lax.fori_loop(first, last, weigh, 0, unroll=4)

    more(0, 8)
    drain(got3.at[:, pl.ds(0, 7)], r3)

    for th in range(2):
        total = got3[th, 0]
        for n in range(1, LINE):
            total = total + got3[th, n]
        half_sum[th] = total
    for i in range(1, LINE):
        send(half_sum.at[0], got4.at[0, z], s4, r4, at(lax.rem(z + i, LINE), y, c))
        send(half_sum.at[1], got4.at[1, y], s4, r4, at(z, lax.rem(y + i, LINE), c))
    got4[0, z] = half_sum[0]
    got4[1, y] = half_sum[1]
    more(8, 16)
    drain(got4.at[:, pl.ds(0, 7)], r4)

    for th in range(2):
        total = got4[th, 0]
        for n in range(1, LINE):
            total = total + got4[th, n]
        factor = (1.0 + total / (total + HALF_POINT)).reshape(16, LANES)
        surge_own[th] = factor.astype(BF16)
    for i in range(1, LINE):
        send(surge_own.at[0], surge.at[0, y], s5, r5, at(z, lax.rem(y + i, LINE), c))
        send(surge_own.at[1], surge.at[1, z], s5, r5, at(lax.rem(z + i, LINE), y, c))
    surge[0, y] = surge_own[0]
    surge[1, z] = surge_own[1]
    more(16, 24)
    drain(surge.at[:, pl.ds(0, 7)], r5)

    factors = [surge[th].reshape(COUNTIES * HALF, LANES) for th in range(2)]
    both = jnp.concatenate(factors, axis=1)

    def apply(g, total):
        columns = pl.ds(pl.multiple_of(g * WIDE, WIDE), WIDE)
        found = jnp.dot(both, hot[:, columns], preferred_element_type=F32)
        tiles = jnp.concatenate([weight[g * 2], weight[g * 2 + 1]], axis=1)
        return total + found.reshape(COUNTIES, HALF, WIDE) * tiles[None]

    total = lax.fori_loop(0, GROUPS, apply, jnp.zeros((COUNTIES, HALF, WIDE), F32), unroll=2)

    for bh in range(2):
        county = jnp.broadcast_to(b_county[bh], (HALF, LANES))
        loss = jnp.zeros((HALF, LANES), F32)
        for n in range(COUNTIES):
            loss = loss + jnp.where(county == n, total[n, :, bh * LANES : (bh + 1) * LANES], 0.0)
        masks = pair_masks(b_tract[bh] & 15, bh)
        left = loss
        for piece in range(3):
            rounded = left.astype(BF16)
            left = left - rounded.astype(F32)
            twice = jnp.concatenate([rounded.astype(F32)] * 2, axis=0).astype(BF16)
            for n in range(8):
                terms[n * 16 : (n + 1) * 16, piece * WIDE + bh * LANES : piece * WIDE + (bh + 1) * LANES] = (
                    twice * masks[n]
                )

    tract_part[...] = lax.dot_general(dest[...], terms[...], NT, preferred_element_type=F32).reshape(16, LINE, LANES)

    send(tract_part.at[y * 2 + 1 - c], got6.at[c * LINE + y], s6, r6, at(z, y, 1 - c))
    for i in range(1, LINE):
        yy = lax.rem(y + i, LINE)
        for h in range(2):
            send(tract_part.at[yy * 2 + h], got6.at[c * LINE + y], s6, r6, at(z, yy, h))
    got6[c * LINE + y] = tract_part[y * 2 + c]
    drain(got6.at[pl.ds(0, 15)], r6)

    for h in range(2):
        total = got6[h * LINE]
        for n in range(1, LINE):
            total = total + got6[h * LINE + n]
        for n in range(LINE):
            rows[n, h : h + 1, :] = total[n : n + 1]
    for i in range(1, LINE):
        zz = lax.rem(z + i, LINE)
        send(rows.at[zz], got7.at[z], s7, r7, at(zz, y, c))
    got7[z] = rows[z]
    drain(got7.at[pl.ds(0, 7)], r7)
    final = got7[0]
    for n in range(1, LINE):
        final = final + got7[n]

    row[...] = final[0:1] + final[1:2]
    for i in range(1, 4):
        send(row, got8.at[x], s8, r8, {"real": lax.rem(x + i, 4)})
    got8[x] = row[...]

    lane = lax.broadcasted_iota(jnp.int32, (16, LANES), 1)
    where_tract = lane // HALF == lax.broadcasted_iota(jnp.int32, (16, LANES), 0)
    from_lane = lax.broadcasted_iota(jnp.int32, (LANES, 16), 0)
    to_lane = lax.broadcasted_iota(jnp.int32, (LANES, 16), 1)
    result = jnp.zeros((16, 16), F32)
    for h in range(2):
        picked = jnp.where(where_tract, jnp.broadcast_to(final[h : h + 1], (16, LANES)), 0.0)
        put = ((from_lane & (HALF - 1)) + h * HALF == to_lane).astype(F32)
        result = result + jnp.dot(picked, put, precision=HIGHEST, preferred_element_type=F32)
    loss_out[...] = result

    drain(got8.at[pl.ds(0, 3)], r8)
    over = got8[0] + got8[1] + got8[2] + got8[3]
    put = (from_lane // HALF == to_lane).astype(F32)
    avg_out[...] = jnp.dot(over, put, precision=HIGHEST, preferred_element_type=F32) * (1.0 / REALS_ALL)

    drain(got6.at[pl.ds(0, 15)], s1)
    drain(sites.at[:, pl.ds(0, 7)], s2)
    drain(got3.at[:, pl.ds(0, 7)], s3)
    drain(got4.at[:, pl.ds(0, 7)], s4)
    drain(surge.at[:, pl.ds(0, 7)], s5)
    drain(got6.at[pl.ds(0, 15)], s6)
    drain(got7.at[pl.ds(0, 7)], s7)
    drain(got8.at[pl.ds(0, 3)], s8)


def shards(site_ln, site_of, county_of, tract_of, comp_type, comp_qty, amplify, frag_median, frag_step, frag_beta, state_cost):
    vmem = pltpu.VMEM
    i32 = jnp.int32
    dma = pltpu.SemaphoreType.DMA
    scratch = [
        vmem((2, 1, LANES), i32), vmem((2, 1, LANES), i32), vmem((2, 1, LANES), i32),
        vmem((2, GROUPS, LANES), i32), vmem((2, GROUPS, LANES), i32), vmem((2, GROUPS, LANES), F32),
        vmem((2, LANES), F32), vmem((2, LANES), F32), vmem((2, LANES), F32), vmem((3, TYPES), F32),
        vmem((2, LINE, LINE, HALF, LANES), F32),
    ]
    scratch += [vmem((2, GROUPS, LANES), F32)] * 7
    scratch += [
        vmem((TYPES, GROUPS * WIDE), BF16), vmem((LANES, GROUPS * WIDE), BF16),
        vmem((2 * GROUPS, HALF, LANES), F32), vmem((2 * GROUPS, HALF, LANES), F32),
        vmem((2, COUNTIES, HALF, LANES), F32), vmem((2, LINE, 2, HALF, LANES), F32),
        vmem((2, 2, HALF, LANES), F32), vmem((2, LINE, 2, HALF, LANES), F32),
        vmem((2, 16, LANES), BF16), vmem((2, LINE, 16, LANES), BF16),
        vmem((LANES, 3 * WIDE), BF16), vmem((LANES, 3 * WIDE), BF16),
        vmem((16, LINE, LANES), F32), vmem((16, LINE, LANES), F32),
        vmem((LINE, 2, LANES), F32), vmem((LINE, 2, LANES), F32),
        vmem((1, LANES), F32), vmem((4, 1, LANES), F32),
    ]
    scratch += [dma((6,)), dma((4,)), dma((6,)), dma((6,))]
    scratch += [dma, dma((2,)), dma, dma((2, LINE))] + [dma] * 12
    loss, avg = pl.pallas_call(
        kernel,
        out_shape=(jax.ShapeDtypeStruct((16, 16), F32), jax.ShapeDtypeStruct((1, 16), F32)),
        in_specs=[pl.BlockSpec(memory_space=pl.ANY)] * 11,
        out_specs=(pl.BlockSpec(memory_space=pltpu.VMEM),) * 2,
        scratch_shapes=scratch,
        compiler_params=pltpu.CompilerParams(
            collective_id=0, has_side_effects=True, vmem_limit_bytes=40 * 1024 * 1024
        ),
    )(
        site_ln, site_of.reshape(1, LANES), county_of.reshape(1, LANES), tract_of.reshape(1, LANES),
        comp_type, comp_qty, amplify,
        frag_median.reshape(2, LANES), frag_step.reshape(2, LANES), frag_beta.reshape(2, LANES), state_cost,
    )
    return loss, avg.reshape(16)


def solution(mesh):
    in_specs = (
        P("real", "bld"), P("bld"), P("bld"), P("bld"), P(None, "bld"), P(None, "bld"), P(None, "bld"),
        P(), P(), P(), P(),
    )
    out_specs = (P("bld", "real"), P("bld"))
    return jax.shard_map(shards, mesh=mesh, in_specs=in_specs, out_specs=out_specs, check_vma=False)
```

```python
import jax
import jax.numpy as jnp
from jax import lax
from jax.experimental import pallas as pl
from jax.experimental.pallas import tpu as pltpu
from jax.sharding import PartitionSpec as P

LINE = 8
GROUPS = 24
TYPES = 256
COUNTIES = 16
LANES = 128
HALF = 8
WIDE = 2 * LANES
REALS_ALL = 64.0
HALF_POINT = 385.0
ROOT_HALF = 0.7071067811865476
MESH = pl.DeviceIdType.MESH
F32 = jnp.float32
BF16 = jnp.bfloat16
HIGHEST = lax.Precision.HIGHEST
NT = (((1,), (1,)), ((), ()))
FAR_FIRST = (4, 3, 5, 2, 6, 1, 7)


def lanes_of(table, index):
    return jnp.take_along_axis(table, index, axis=1, mode="promise_in_bounds")


def drain(ref, sem):
    pltpu.make_async_copy(ref, ref, sem).wait()


def kernel(
    site_ln, site_of, county_of, tract_of, comp_type, comp_qty, amplify,
    frag_median, frag_step, frag_beta, state_cost,
    loss_out, avg_out,
    b_ln, b_site, b_county, b_tract, b_type, b_qty, b_amp,
    t_med, t_step, t_beta, t_cost,
    sites, p_base, p_inv, p_step, p_half, p_c0, p_c1, p_c2,
    hot, spread, args, weight,
    part, got3, half_sum, got4, surge_own, surge,
    dest, terms, tract_part, got6, rows, got7, joint, got8,
    loc_sem, par_sem, bld_send, bld_recv,
    s1, r1, s2, r2, s3, r3, s4, r4, s5, r5, s6, r6, s7, r7, s8, r8,
):
    me = lax.axis_index("bld")
    x = lax.axis_index("real")
    z = me // (2 * LINE)
    y = lax.rem(me // 2, LINE)
    c = lax.rem(me, 2)

    def at(zz, yy, cc):
        return {"bld": (zz * LINE + yy) * 2 + cc}

    def send(src, dst, ssem, rsem, who):
        pltpu.make_async_remote_copy(
            src_ref=src, dst_ref=dst, send_sem=ssem, recv_sem=rsem,
            device_id=who, device_id_type=MESH,
        ).start()

    barrier = pltpu.get_barrier_semaphore()

    def hello(who):
        pl.semaphore_signal(barrier, inc=1, device_id=who, device_id_type=MESH)

    for i in FAR_FIRST:
        for h in range(2):
            hello(at(z, lax.rem(y + i, LINE), h))
            hello(at(lax.rem(z + i, LINE), y, h))
    for i in (2, 1, 3):
        hello({"real": lax.rem(x + i, 4)})
    hello(at(z, y, 1 - c))

    buildings = (
        (site_of, b_site), (county_of, b_county), (tract_of, b_tract),
        (comp_type, b_type), (comp_qty, b_qty), (amplify, b_amp),
    )
    tables = ((frag_median, t_med), (frag_step, t_step), (frag_beta, t_beta), (state_cost, t_cost))
    own = [pltpu.make_async_copy(a, b.at[0], loc_sem.at[n]) for n, (a, b) in enumerate(buildings)]
    own += [pltpu.make_async_copy(a, b, par_sem.at[n]) for n, (a, b) in enumerate(tables)]
    own.append(pltpu.make_async_copy(site_ln, b_ln, par_sem.at[4]))
    for copy in own:
        copy.start()

    pl.semaphore_wait(barrier, 1 + 4 * (LINE - 1) + 3)
    for copy in own:
        copy.wait()

    p = y * (1 - c) + z * c
    q = z * (1 - c) + y * c
    mine = sites.at[c, q, p]
    local = pltpu.make_async_copy(b_ln.at[pl.ds(pl.multiple_of(c * HALF, HALF), HALF)], mine, r1.at[c])
    local.start()
    for i in FAR_FIRST:
        pp = lax.rem(p + i, LINE)
        for h in range(2):
            zz = q * (1 - c) + pp * c
            yy = pp * (1 - c) + q * c
            send(b_ln.at[pl.ds(h * HALF, HALF)], mine, s1, r1.at[c], at(zz, yy, h))
    send(b_ln.at[pl.ds(pl.multiple_of((1 - c) * HALF, HALF), HALF)], mine, s1, r1.at[c], at(z, y, 1 - c))
    trade = [
        pltpu.make_async_remote_copy(
            src_ref=b.at[0], dst_ref=b.at[1], send_sem=bld_send.at[n], recv_sem=bld_recv.at[n],
            device_id=at(z, y, 1 - c), device_id_type=MESH,
        )
        for n, (a, b) in enumerate(buildings)
    ]
    for copy in trade:
        copy.start()

    drain(sites.at[0, z], r1.at[0])
    for i in FAR_FIRST:
        send(sites.at[0, z], sites.at[0, z], s2, r2.at[0, i], at(lax.rem(z + i, LINE), y, c))
    drain(sites.at[1, y], r1.at[1])
    for i in FAR_FIRST:
        send(sites.at[1, y], sites.at[1, y], s2, r2.at[1, i], at(z, lax.rem(y + i, LINE), c))

    for copy in trade:
        copy.wait()
    inv_row = ROOT_HALF / t_beta[...]
    step_row = t_step[...] * inv_row
    med_row = t_med[...]
    cost = t_cost[...]

    def cost_rows(level):
        now = cost[level : level + 1]
        if level:
            now = now - cost[level - 1 : level]
        return now[:, :LANES], now[:, LANES:]

    def pair(table):
        return table[0:1], table[1:2]

    looked = (
        (pair(med_row), p_base), (pair(inv_row), p_inv), (pair(step_row), p_step),
        (cost_rows(0), p_c0), (cost_rows(1), p_c1), (cost_rows(2), p_c2),
    )
    for bh in range(2):
        for g in range(0, GROUPS, 8):
            index = b_type[bh, g : g + 8, :]
            low = index & (LANES - 1)
            high = index >= LANES
            for (first, second), into in looked:
                value = jnp.where(
                    high,
                    lanes_of(jnp.broadcast_to(second, (8, LANES)), low),
                    lanes_of(jnp.broadcast_to(first, (8, LANES)), low),
                )
                if into is p_base:
                    value = b_amp[bh, g : g + 8, :] - value
                into[bh, g : g + 8, :] = value
            p_half[bh, g : g + 8, :] = 0.5 * b_qty[bh, g : g + 8, :].astype(F32)

    one = jnp.ones((16, LANES), BF16)
    zero = jnp.zeros((16, LANES), BF16)
    count = lax.broadcasted_iota(jnp.int32, (16, LANES), 0)

    counts = [(count + 16 * n).astype(F32).astype(BF16) for n in range(TYPES // 16)]

    def make_hot(g, _):
        for bh in range(2):
            types = jnp.broadcast_to(b_type[bh, pl.ds(g, 1), :], (16, LANES)).astype(F32).astype(BF16)
            columns = pl.ds(pl.multiple_of(g * WIDE + bh * LANES, LANES), LANES)
            for n in range(TYPES // 16):
                hot[n * 16 : (n + 1) * 16, columns] = jnp.where(types == counts[n], one, zero)
        return 0

    lax.fori_loop(0, GROUPS, make_hot, 0)

    for bh in range(2):
        owner = b_tract[bh] // 16
        place = (owner & 15) * LINE + owner // 16
        place = jnp.broadcast_to(place, (16, LANES)).astype(F32).astype(BF16)
        for n in range(8):
            value = jnp.where(place == counts[n], one, zero)
            for piece in range(3):
                dest[n * 16 : (n + 1) * 16, piece * WIDE + bh * LANES : piece * WIDE + (bh + 1) * LANES] = value

    upper = (count >= HALF).astype(jnp.int32)

    def pair_masks(ref, bh):
        value = jnp.broadcast_to(ref, (16, LANES)) - upper
        value = value.astype(F32).astype(BF16)
        return [jnp.where(value == jnp.asarray(2 * n, BF16), one, zero) for n in range(8)]

    low = [jnp.broadcast_to(b_site[bh] & (LANES - 1), (HALF, LANES)) for bh in range(2)]
    high = [jnp.broadcast_to(b_site[bh] // LANES, (HALF, LANES)) for bh in range(2)]
    level = [jnp.zeros((HALF, LANES), F32) for _ in range(2)]

    def pick(level, route, line):
        for n in range(LINE):
            tile = sites[route, line, n]
            block = (line * 16 + 2 * n) if route == 0 else (n * 16 + line * 2 + 1)
            level = [jnp.where(high[bh] == block, lanes_of(tile, low[bh]), level[bh]) for bh in range(2)]
        return level

    level = pick(level, 0, z)
    level = pick(level, 1, y)
    for i in (1, 7, 2, 6, 3, 5, 4):
        zz = lax.rem(z + LINE - i, LINE)
        drain(sites.at[0, zz], r2.at[0, i])
        level = pick(level, 0, zz)
        yy = lax.rem(y + LINE - i, LINE)
        drain(sites.at[1, yy], r2.at[1, i])
        level = pick(level, 1, yy)

    for bh in range(2):
        masks = pair_masks(b_county[bh], bh)

        def damage(g, _):
            row_at = pl.ds(g, 1)
            arg = (level[bh] + p_base[bh, row_at, :]) * p_inv[bh, row_at, :]
            dam = p_half[bh, row_at, :] * (1.0 + lax.erf(arg))
            args[g * 2 + bh] = arg
            weight[g * 2 + bh] = dam * p_c0[bh, row_at, :]
            twice = jnp.concatenate([dam, dam], axis=0).astype(BF16)
            columns = pl.ds(pl.multiple_of(g * WIDE + bh * LANES, LANES), LANES)
            for n in range(8):
                spread[n * 16 : (n + 1) * 16, columns] = twice * masks[n]
            return 0

        lax.fori_loop(0, GROUPS, damage, 0, unroll=4)

    sums = lax.dot_general(spread[...], hot[...], NT, preferred_element_type=F32)
    part[0] = sums[:, :LANES].reshape(COUNTIES, HALF, LANES)
    part[1] = sums[:, LANES:].reshape(COUNTIES, HALF, LANES)

    for i in FAR_FIRST:
        yy = lax.rem(y + i, LINE)
        send(part.at[0, pl.ds(2 * yy, 2)], got3.at[0, y], s3, r3, at(z, yy, c))
        zz = lax.rem(z + i, LINE)
        send(part.at[1, pl.ds(2 * zz, 2)], got3.at[1, z], s3, r3, at(zz, y, c))
    got3[0, y] = part[0, pl.ds(2 * y, 2)]
    got3[1, z] = part[1, pl.ds(2 * z, 2)]

    def more(first, last):
        def weigh(g, _):
            row_at = pl.ds(g, 1)
            for bh in range(2):
                arg = args[g * 2 + bh]
                step = p_step[bh, row_at, :]
                rest = (1.0 + lax.erf(arg - step)) * p_c1[bh, row_at, :]
                rest = rest + (1.0 + lax.erf(arg - 2.0 * step)) * p_c2[bh, row_at, :]
                weight[g * 2 + bh] = weight[g * 2 + bh] + p_half[bh, row_at, :] * rest
            return 0

        lax.fori_loop(first, last, weigh, 0, unroll=4)

    more(0, 8)
    drain(got3.at[:, pl.ds(0, 7)], r3)

    for th in range(2):
        total = got3[th, 0]
        for n in range(1, LINE):
            total = total + got3[th, n]
        half_sum[th] = total
    for i in FAR_FIRST:
        send(half_sum.at[0], got4.at[0, z], s4, r4, at(lax.rem(z + i, LINE), y, c))
        send(half_sum.at[1], got4.at[1, y], s4, r4, at(z, lax.rem(y + i, LINE), c))
    got4[0, z] = half_sum[0]
    got4[1, y] = half_sum[1]
    more(8, 16)
    drain(got4.at[:, pl.ds(0, 7)], r4)

    for th in range(2):
        total = got4[th, 0]
        for n in range(1, LINE):
            total = total + got4[th, n]
        factor = (1.0 + total / (total + HALF_POINT)).reshape(16, LANES)
        surge_own[th] = factor.astype(BF16)
    for i in FAR_FIRST:
        send(surge_own.at[0], surge.at[0, y], s5, r5, at(z, lax.rem(y + i, LINE), c))
        send(surge_own.at[1], surge.at[1, z], s5, r5, at(lax.rem(z + i, LINE), y, c))
    surge[0, y] = surge_own[0]
    surge[1, z] = surge_own[1]
    more(16, 24)
    drain(surge.at[:, pl.ds(0, 7)], r5)

    factors = [surge[th].reshape(COUNTIES * HALF, LANES) for th in range(2)]
    both = jnp.concatenate(factors, axis=1)

    def apply(g, total):
        columns = pl.ds(pl.multiple_of(g * WIDE, WIDE), WIDE)
        found = jnp.dot(both, hot[:, columns], preferred_element_type=F32)
        tiles = jnp.concatenate([weight[g * 2], weight[g * 2 + 1]], axis=1)
        return total + found.reshape(COUNTIES, HALF, WIDE) * tiles[None]

    total = lax.fori_loop(0, GROUPS, apply, jnp.zeros((COUNTIES, HALF, WIDE), F32), unroll=2)

    for bh in range(2):
        county = jnp.broadcast_to(b_county[bh], (HALF, LANES))
        loss = jnp.zeros((HALF, LANES), F32)
        for n in range(COUNTIES):
            loss = loss + jnp.where(county == n, total[n, :, bh * LANES : (bh + 1) * LANES], 0.0)
        masks = pair_masks(b_tract[bh] & 15, bh)
        left = loss
        for piece in range(3):
            rounded = left.astype(BF16)
            left = left - rounded.astype(F32)
            twice = jnp.concatenate([rounded.astype(F32)] * 2, axis=0).astype(BF16)
            for n in range(8):
                terms[n * 16 : (n + 1) * 16, piece * WIDE + bh * LANES : piece * WIDE + (bh + 1) * LANES] = (
                    twice * masks[n]
                )

    tract_part[...] = lax.dot_general(dest[...], terms[...], NT, preferred_element_type=F32).reshape(16, LINE, LANES)

    for i in FAR_FIRST:
        yy = lax.rem(y + i, LINE)
        for h in range(2):
            send(tract_part.at[yy * 2 + h], got6.at[c * LINE + y], s6, r6, at(z, yy, h))
    send(tract_part.at[y * 2 + 1 - c], got6.at[c * LINE + y], s6, r6, at(z, y, 1 - c))
    got6[c * LINE + y] = tract_part[y * 2 + c]
    drain(got6.at[pl.ds(0, 15)], r6)

    halves = []
    for h in range(2):
        total = got6[h * LINE]
        for n in range(1, LINE):
            total = total + got6[h * LINE + n]
        halves.append(total)
        for n in range(LINE):
            rows[n, h : h + 1, :] = total[n : n + 1]
    total = halves[0] + halves[1]
    for n in range(LINE):
        joint[n] = total[n : n + 1]
    for i, k in ((4, 2), (4, 1), (4, 3), (3, 2), (5, 2), (4, 0), (3, 1), (3, 3), (5, 1), (5, 3), (2, 2), (6, 2), (3, 0), (5, 0),
                 (2, 1), (2, 3), (6, 1), (6, 3), (1, 2), (7, 2), (2, 0), (6, 0), (1, 1), (1, 3), (7, 1), (7, 3), (0, 2),
                 (1, 0), (7, 0), (0, 1), (0, 3)):
        zz = lax.rem(z + i, LINE)
        if k == 0:
            send(rows.at[zz], got7.at[z], s7, r7, at(zz, y, c))
        else:
            who = {"bld": (zz * LINE + y) * 2 + c, "real": lax.rem(x + k, 4)}
            send(joint.at[zz], got8.at[(k - 1) * LINE + z], s8, r8, who)
    got7[z] = rows[z]
    drain(got7.at[pl.ds(0, 7)], r7)
    final = got7[0]
    for n in range(1, LINE):
        final = final + got7[n]

    lane = lax.broadcasted_iota(jnp.int32, (16, LANES), 1)
    where_tract = lane // HALF == lax.broadcasted_iota(jnp.int32, (16, LANES), 0)
    from_lane = lax.broadcasted_iota(jnp.int32, (LANES, 16), 0)
    to_lane = lax.broadcasted_iota(jnp.int32, (LANES, 16), 1)
    result = jnp.zeros((16, 16), F32)
    for h in range(2):
        picked = jnp.where(where_tract, jnp.broadcast_to(final[h : h + 1], (16, LANES)), 0.0)
        put = ((from_lane & (HALF - 1)) + h * HALF == to_lane).astype(F32)
        result = result + jnp.dot(picked, put, precision=HIGHEST, preferred_element_type=F32)
    loss_out[...] = result

    drain(got8, r8)
    over = final[0:1] + final[1:2]
    for n in range(3 * LINE):
        over = over + got8[n]
    put = (from_lane // HALF == to_lane).astype(F32)
    avg_out[...] = jnp.dot(over, put, precision=HIGHEST, preferred_element_type=F32) * (1.0 / REALS_ALL)

    drain(got6.at[pl.ds(0, 15)], s1)
    drain(sites.at[:, pl.ds(0, 7)], s2)
    drain(got3.at[:, pl.ds(0, 7)], s3)
    drain(got4.at[:, pl.ds(0, 7)], s4)
    drain(surge.at[:, pl.ds(0, 7)], s5)
    drain(got6.at[pl.ds(0, 15)], s6)
    drain(got7.at[pl.ds(0, 7)], s7)
    drain(got8, s8)


def shards(site_ln, site_of, county_of, tract_of, comp_type, comp_qty, amplify, frag_median, frag_step, frag_beta, state_cost):
    vmem = pltpu.VMEM
    i32 = jnp.int32
    dma = pltpu.SemaphoreType.DMA
    scratch = [
        vmem((2 * HALF, LANES), F32),
        vmem((2, 1, LANES), i32), vmem((2, 1, LANES), i32), vmem((2, 1, LANES), i32),
        vmem((2, GROUPS, LANES), i32), vmem((2, GROUPS, LANES), i32), vmem((2, GROUPS, LANES), F32),
        vmem((2, LANES), F32), vmem((2, LANES), F32), vmem((2, LANES), F32), vmem((3, TYPES), F32),
        vmem((2, LINE, LINE, HALF, LANES), F32),
    ]
    scratch += [vmem((2, GROUPS, LANES), F32)] * 7
    scratch += [
        vmem((TYPES, GROUPS * WIDE), BF16), vmem((LANES, GROUPS * WIDE), BF16),
        vmem((2 * GROUPS, HALF, LANES), F32), vmem((2 * GROUPS, HALF, LANES), F32),
        vmem((2, COUNTIES, HALF, LANES), F32), vmem((2, LINE, 2, HALF, LANES), F32),
        vmem((2, 2, HALF, LANES), F32), vmem((2, LINE, 2, HALF, LANES), F32),
        vmem((2, 16, LANES), BF16), vmem((2, LINE, 16, LANES), BF16),
        vmem((LANES, 3 * WIDE), BF16), vmem((LANES, 3 * WIDE), BF16),
        vmem((16, LINE, LANES), F32), vmem((16, LINE, LANES), F32),
        vmem((LINE, 2, LANES), F32), vmem((LINE, 2, LANES), F32),
        vmem((LINE, 1, LANES), F32), vmem((3 * LINE, 1, LANES), F32),
    ]
    scratch += [dma((6,)), dma((5,)), dma((6,)), dma((6,))]
    scratch += [dma, dma((2,)), dma, dma((2, LINE))] + [dma] * 12
    loss, avg = pl.pallas_call(
        kernel,
        out_shape=(jax.ShapeDtypeStruct((16, 16), F32), jax.ShapeDtypeStruct((1, 16), F32)),
        in_specs=[pl.BlockSpec(memory_space=pltpu.HBM)] * 11,
        out_specs=(pl.BlockSpec(memory_space=pltpu.VMEM),) * 2,
        scratch_shapes=scratch,
        compiler_params=pltpu.CompilerParams(
            collective_id=0, has_side_effects=True, vmem_limit_bytes=56 * 1024 * 1024
        ),
    )(
        site_ln, site_of.reshape(1, LANES), county_of.reshape(1, LANES), tract_of.reshape(1, LANES),
        comp_type, comp_qty, amplify,
        frag_median.reshape(2, LANES), frag_step.reshape(2, LANES), frag_beta.reshape(2, LANES), state_cost,
    )
    return loss, avg.reshape(16)


def solution(mesh):
    in_specs = (
        P("real", "bld"), P("bld"), P("bld"), P("bld"), P(None, "bld"), P(None, "bld"), P(None, "bld"),
        P(), P(), P(), P(),
    )
    out_specs = (P("bld", "real"), P("bld"))
    return jax.shard_map(shards, mesh=mesh, in_specs=in_specs, out_specs=out_specs, check_vma=False)
```

```python
import jax
import jax.numpy as jnp
from jax import lax
from jax.experimental import pallas as pl
from jax.experimental.pallas import tpu as pltpu
from jax.sharding import PartitionSpec as P

LINE = 8
GROUPS = 24
TYPES = 256
COUNTIES = 16
LANES = 128
HALF = 8
WIDE = 2 * LANES
REALS_ALL = 64.0
HALF_POINT = 385.0
ROOT_HALF = 0.7071067811865476
MESH = pl.DeviceIdType.MESH
F32 = jnp.float32
BF16 = jnp.bfloat16
HIGHEST = lax.Precision.HIGHEST
NT = (((1,), (1,)), ((), ()))
QUARTER = 4
STEPS = 65535.0 / 8.0
FAR_FIRST = (4, 3, 5, 2, 6, 1, 7)
CHUNK = 4


def lanes_of(table, index):
    return jnp.take_along_axis(table, index, axis=1, mode="promise_in_bounds")


def drain(ref, sem):
    pltpu.make_async_copy(ref, ref, sem).wait()


def kernel(
    site_ln, site_of, county_of, tract_of, comp_type, comp_qty, amplify,
    frag_median, frag_step, frag_beta, state_cost,
    loss_out, avg_out,
    b_ln, packed, b_site, b_county, b_tract, b_type, b_qty, b_amp,
    t_med, t_step, t_beta, t_cost,
    sites, p_base, p_inv, p_step, p_half, p_c0, p_c1, p_c2,
    hot, spread, args, weight,
    part, got3, half_sum, got4, surge_own, surge,
    dest, terms, tract_part, got6, rows, got7, joint, got8,
    loc_sem, par_sem, bld_send, bld_recv,
    s1, r1, s2, r2, s3, r3, s4, r4, s5, r5, s6, r6, s7, r7, s8, r8,
):
    me = lax.axis_index("bld")
    x = lax.axis_index("real")
    z = me // (2 * LINE)
    y = lax.rem(me // 2, LINE)
    c = lax.rem(me, 2)

    def at(zz, yy, cc):
        return {"bld": (zz * LINE + yy) * 2 + cc}

    def send(src, dst, ssem, rsem, who):
        pltpu.make_async_remote_copy(
            src_ref=src, dst_ref=dst, send_sem=ssem, recv_sem=rsem,
            device_id=who, device_id_type=MESH,
        ).start()

    barrier = pltpu.get_barrier_semaphore()

    def hello(who):
        pl.semaphore_signal(barrier, inc=1, device_id=who, device_id_type=MESH)

    for i in FAR_FIRST:
        for h in range(2):
            hello(at(z, lax.rem(y + i, LINE), h))
            hello(at(lax.rem(z + i, LINE), y, h))
    for i in (2, 1, 3):
        hello({"real": lax.rem(x + i, 4)})
    hello(at(z, y, 1 - c))

    buildings = (
        (site_of, b_site), (county_of, b_county), (tract_of, b_tract),
        (comp_type, b_type), (comp_qty, b_qty), (amplify, b_amp),
    )
    tables = ((frag_median, t_med), (frag_step, t_step), (frag_beta, t_beta), (state_cost, t_cost))
    own = [pltpu.make_async_copy(a, b.at[0], loc_sem.at[n]) for n, (a, b) in enumerate(buildings)]
    own += [pltpu.make_async_copy(a, b, par_sem.at[n]) for n, (a, b) in enumerate(tables)]
    own.append(pltpu.make_async_copy(site_ln, b_ln, par_sem.at[4]))
    for copy in own:
        copy.start()

    for copy in own:
        copy.wait()
    fixed = ((b_ln[...] + 4.0) * STEPS + 0.5).astype(jnp.int32)
    for h in range(2):
        first = h * HALF
        packed[h] = fixed[first : first + QUARTER] | (fixed[first + QUARTER : first + HALF] << 16)
    pl.semaphore_wait(barrier, 1 + 4 * (LINE - 1) + 3)

    p = y * (1 - c) + z * c
    q = z * (1 - c) + y * c
    mine = sites.at[c, q, p]
    local = pltpu.make_async_copy(packed.at[c], mine, r1.at[c])
    local.start()
    for i in FAR_FIRST:
        pp = lax.rem(p + i, LINE)
        for h in range(2):
            zz = q * (1 - c) + pp * c
            yy = pp * (1 - c) + q * c
            send(packed.at[h], mine, s1, r1.at[c], at(zz, yy, h))
    send(packed.at[1 - c], mine, s1, r1.at[c], at(z, y, 1 - c))
    trade = [
        pltpu.make_async_remote_copy(
            src_ref=b.at[0], dst_ref=b.at[1], send_sem=bld_send.at[n], recv_sem=bld_recv.at[n],
            device_id=at(z, y, 1 - c), device_id_type=MESH,
        )
        for n, (a, b) in enumerate(buildings)
    ]
    for copy in trade:
        copy.start()

    drain(sites.at[0, z], r1.at[0])
    for i in FAR_FIRST:
        send(sites.at[0, z], sites.at[0, z], s2, r2.at[0, i], at(lax.rem(z + i, LINE), y, c))
    drain(sites.at[1, y], r1.at[1])
    for i in FAR_FIRST:
        send(sites.at[1, y], sites.at[1, y], s2, r2.at[1, i], at(z, lax.rem(y + i, LINE), c))

    for copy in trade:
        copy.wait()
    inv_row = ROOT_HALF / t_beta[...]
    step_row = t_step[...] * inv_row
    med_row = t_med[...]
    cost = t_cost[...]

    def cost_rows(level):
        now = cost[level : level + 1]
        if level:
            now = now - cost[level - 1 : level]
        return now[:, :LANES], now[:, LANES:]

    def pair(table):
        return table[0:1], table[1:2]

    looked = (
        (pair(med_row), p_base), (pair(inv_row), p_inv), (pair(step_row), p_step),
        (cost_rows(0), p_c0), (cost_rows(1), p_c1), (cost_rows(2), p_c2),
    )
    for bh in range(2):
        for g in range(0, GROUPS, 8):
            index = b_type[bh, g : g + 8, :]
            low = index & (LANES - 1)
            high = index >= LANES
            for (first, second), into in looked:
                value = jnp.where(
                    high,
                    lanes_of(jnp.broadcast_to(second, (8, LANES)), low),
                    lanes_of(jnp.broadcast_to(first, (8, LANES)), low),
                )
                if into is p_base:
                    value = b_amp[bh, g : g + 8, :] - value
                into[bh, g : g + 8, :] = value
            p_half[bh, g : g + 8, :] = 0.5 * b_qty[bh, g : g + 8, :].astype(F32)

    one = jnp.ones((16, LANES), BF16)
    zero = jnp.zeros((16, LANES), BF16)
    count = lax.broadcasted_iota(jnp.int32, (16, LANES), 0)

    counts = [(count + 16 * n).astype(F32).astype(BF16) for n in range(TYPES // 16)]

    def make_hot(g, _):
        for bh in range(2):
            types = jnp.broadcast_to(b_type[bh, pl.ds(g, 1), :], (16, LANES)).astype(F32).astype(BF16)
            columns = pl.ds(pl.multiple_of(g * WIDE + bh * LANES, LANES), LANES)
            for n in range(TYPES // 16):
                hot[n * 16 : (n + 1) * 16, columns] = jnp.where(types == counts[n], one, zero)
        return 0

    lax.fori_loop(0, GROUPS, make_hot, 0)

    for bh in range(2):
        owner = b_tract[bh] // 16
        place = (owner & 15) * LINE + owner // 16
        place = jnp.broadcast_to(place, (16, LANES)).astype(F32).astype(BF16)
        for n in range(8):
            value = jnp.where(place == counts[n], one, zero)
            for piece in range(3):
                dest[n * 16 : (n + 1) * 16, piece * WIDE + bh * LANES : piece * WIDE + (bh + 1) * LANES] = value

    upper = (count >= HALF).astype(jnp.int32)

    def pair_masks(ref, bh):
        value = jnp.broadcast_to(ref, (16, LANES)) - upper
        value = value.astype(F32).astype(BF16)
        return [jnp.where(value == jnp.asarray(2 * n, BF16), one, zero) for n in range(8)]

    low = [jnp.broadcast_to(b_site[bh] & (LANES - 1), (HALF, LANES)) for bh in range(2)]
    high = [jnp.broadcast_to(b_site[bh] // LANES, (HALF, LANES)) for bh in range(2)]
    second = (lax.broadcasted_iota(jnp.int32, (HALF, LANES), 0) >= QUARTER).astype(jnp.int32)
    apart = [[high[bh] - second * stride for bh in range(2)] for stride in (2, 16)]
    level = [jnp.zeros((HALF, LANES), jnp.int32) for _ in range(2)]

    def pick(level, route, line):
        for n in range(0, LINE, 2):
            tile = jnp.concatenate([sites[route, line, n], sites[route, line, n + 1]], axis=0)
            block = (line * 16 + 2 * n) if route == 0 else (n * 16 + line * 2 + 1)
            level = [
                jnp.where(apart[route][bh] == block, lanes_of(tile, low[bh]), level[bh]) for bh in range(2)
            ]
        return level

    level = pick(level, 0, z)
    level = pick(level, 1, y)
    for i in (1, 7, 2, 6, 3, 5, 4):
        zz = lax.rem(z + LINE - i, LINE)
        drain(sites.at[0, zz], r2.at[0, i])
        level = pick(level, 0, zz)
        yy = lax.rem(y + LINE - i, LINE)
        drain(sites.at[1, yy], r2.at[1, i])
        level = pick(level, 1, yy)

    for bh in range(2):
        word = level[bh][:QUARTER] | level[bh][QUARTER:]
        both_halves = jnp.concatenate([word & 0xFFFF, (word >> 16) & 0xFFFF], axis=0)
        level[bh] = both_halves.astype(F32) * (1.0 / STEPS) - 4.0

    county_masks = [pair_masks(b_county[bh], bh) for bh in range(2)]
    sums = None
    for j in range(GROUPS // CHUNK + 1):
        if j < GROUPS // CHUNK:
            for g in range(j * CHUNK, (j + 1) * CHUNK):
                for bh in range(2):
                    arg = (level[bh] + p_base[bh, g : g + 1, :]) * p_inv[bh, g : g + 1, :]
                    dam = p_half[bh, g : g + 1, :] * (1.0 + lax.erf(arg))
                    args[g * 2 + bh] = arg
                    weight[g * 2 + bh] = dam * p_c0[bh, g : g + 1, :]
                    twice = jnp.concatenate([dam, dam], axis=0).astype(BF16)
                    first = g * WIDE + bh * LANES
                    for n in range(8):
                        spread[n * 16 : (n + 1) * 16, first : first + LANES] = twice * county_masks[bh][n]
        if j:
            columns = slice((j - 1) * CHUNK * WIDE, j * CHUNK * WIDE)
            found = lax.dot_general(spread[:, columns], hot[:, columns], NT, preferred_element_type=F32)
            sums = found if sums is None else sums + found

    part[0] = sums[:, :LANES].reshape(COUNTIES, HALF, LANES)
    part[1] = sums[:, LANES:].reshape(COUNTIES, HALF, LANES)

    for i in FAR_FIRST:
        yy = lax.rem(y + i, LINE)
        send(part.at[0, pl.ds(2 * yy, 2)], got3.at[0, y], s3, r3, at(z, yy, c))
        zz = lax.rem(z + i, LINE)
        send(part.at[1, pl.ds(2 * zz, 2)], got3.at[1, z], s3, r3, at(zz, y, c))
    got3[0, y] = part[0, pl.ds(2 * y, 2)]
    got3[1, z] = part[1, pl.ds(2 * z, 2)]

    def more(first, last):
        def weigh(g, _):
            row_at = pl.ds(g, 1)
            for bh in range(2):
                arg = args[g * 2 + bh]
                step = p_step[bh, row_at, :]
                rest = (1.0 + lax.erf(arg - step)) * p_c1[bh, row_at, :]
                rest = rest + (1.0 + lax.erf(arg - 2.0 * step)) * p_c2[bh, row_at, :]
                weight[g * 2 + bh] = weight[g * 2 + bh] + p_half[bh, row_at, :] * rest
            return 0

        lax.fori_loop(first, last, weigh, 0, unroll=4)

    more(0, 8)
    drain(got3.at[:, pl.ds(0, 7)], r3)

    for th in range(2):
        total = got3[th, 0]
        for n in range(1, LINE):
            total = total + got3[th, n]
        half_sum[th] = total
    for i in FAR_FIRST:
        send(half_sum.at[0], got4.at[0, z], s4, r4, at(lax.rem(z + i, LINE), y, c))
        send(half_sum.at[1], got4.at[1, y], s4, r4, at(z, lax.rem(y + i, LINE), c))
    got4[0, z] = half_sum[0]
    got4[1, y] = half_sum[1]
    more(8, 16)
    drain(got4.at[:, pl.ds(0, 7)], r4)

    for th in range(2):
        total = got4[th, 0]
        for n in range(1, LINE):
            total = total + got4[th, n]
        factor = (1.0 + total / (total + HALF_POINT)).reshape(16, LANES)
        surge_own[th] = factor.astype(BF16)
    for i in FAR_FIRST:
        send(surge_own.at[0], surge.at[0, y], s5, r5, at(z, lax.rem(y + i, LINE), c))
        send(surge_own.at[1], surge.at[1, z], s5, r5, at(lax.rem(z + i, LINE), y, c))
    surge[0, y] = surge_own[0]
    surge[1, z] = surge_own[1]
    more(16, 24)
    drain(surge.at[:, pl.ds(0, 7)], r5)

    factors = [surge[th].reshape(COUNTIES * HALF, LANES) for th in range(2)]
    both = jnp.concatenate(factors, axis=1)

    def apply(g, total):
        columns = pl.ds(pl.multiple_of(g * WIDE, WIDE), WIDE)
        found = jnp.dot(both, hot[:, columns], preferred_element_type=F32)
        tiles = jnp.concatenate([weight[g * 2], weight[g * 2 + 1]], axis=1)
        return total + found.reshape(COUNTIES, HALF, WIDE) * tiles[None]

    total = lax.fori_loop(0, GROUPS, apply, jnp.zeros((COUNTIES, HALF, WIDE), F32), unroll=8)

    for bh in range(2):
        county = jnp.broadcast_to(b_county[bh], (HALF, LANES))
        loss = jnp.zeros((HALF, LANES), F32)
        for n in range(COUNTIES):
            loss = loss + jnp.where(county == n, total[n, :, bh * LANES : (bh + 1) * LANES], 0.0)
        masks = pair_masks(b_tract[bh] & 15, bh)
        left = loss
        for piece in range(3):
            rounded = left.astype(BF16)
            left = left - rounded.astype(F32)
            twice = jnp.concatenate([rounded.astype(F32)] * 2, axis=0).astype(BF16)
            for n in range(8):
                terms[n * 16 : (n + 1) * 16, piece * WIDE + bh * LANES : piece * WIDE + (bh + 1) * LANES] = (
                    twice * masks[n]
                )

    tract_part[...] = lax.dot_general(dest[...], terms[...], NT, preferred_element_type=F32).reshape(16, LINE, LANES)

    for i in FAR_FIRST:
        yy = lax.rem(y + i, LINE)
        for h in range(2):
            send(tract_part.at[yy * 2 + h], got6.at[c * LINE + y], s6, r6, at(z, yy, h))
    send(tract_part.at[y * 2 + 1 - c], got6.at[c * LINE + y], s6, r6, at(z, y, 1 - c))
    got6[c * LINE + y] = tract_part[y * 2 + c]
    drain(got6.at[pl.ds(0, 15)], r6)

    halves = []
    for h in range(2):
        total = got6[h * LINE]
        for n in range(1, LINE):
            total = total + got6[h * LINE + n]
        halves.append(total)
        for n in range(LINE):
            rows[n, h : h + 1, :] = total[n : n + 1]
    total = halves[0] + halves[1]
    for n in range(LINE):
        joint[n] = total[n : n + 1]
    for i, k in ((4, 2), (4, 1), (4, 3), (3, 2), (5, 2), (4, 0), (3, 1), (3, 3), (5, 1), (5, 3), (2, 2), (6, 2), (3, 0), (5, 0),
                 (2, 1), (2, 3), (6, 1), (6, 3), (1, 2), (7, 2), (2, 0), (6, 0), (1, 1), (1, 3), (7, 1), (7, 3), (0, 2),
                 (1, 0), (7, 0), (0, 1), (0, 3)):
        zz = lax.rem(z + i, LINE)
        if k == 0:
            send(rows.at[zz], got7.at[z], s7, r7, at(zz, y, c))
        else:
            who = {"bld": (zz * LINE + y) * 2 + c, "real": lax.rem(x + k, 4)}
            send(joint.at[zz], got8.at[(k - 1) * LINE + z], s8, r8, who)
    got7[z] = rows[z]
    drain(got7.at[pl.ds(0, 7)], r7)
    final = got7[0]
    for n in range(1, LINE):
        final = final + got7[n]

    lane = lax.broadcasted_iota(jnp.int32, (16, LANES), 1)
    where_tract = lane // HALF == lax.broadcasted_iota(jnp.int32, (16, LANES), 0)
    from_lane = lax.broadcasted_iota(jnp.int32, (LANES, 16), 0)
    to_lane = lax.broadcasted_iota(jnp.int32, (LANES, 16), 1)
    result = jnp.zeros((16, 16), F32)
    for h in range(2):
        picked = jnp.where(where_tract, jnp.broadcast_to(final[h : h + 1], (16, LANES)), 0.0)
        put = ((from_lane & (HALF - 1)) + h * HALF == to_lane).astype(F32)
        result = result + jnp.dot(picked, put, precision=HIGHEST, preferred_element_type=F32)
    loss_out[...] = result

    drain(got8, r8)
    over = final[0:1] + final[1:2]
    for n in range(3 * LINE):
        over = over + got8[n]
    put = (from_lane // HALF == to_lane).astype(F32)
    avg_out[...] = jnp.dot(over, put, precision=HIGHEST, preferred_element_type=F32) * (1.0 / REALS_ALL)

    drain(sites.at[0, pl.ds(0, 3), pl.ds(0, 5)], s1)
    drain(sites.at[:, pl.ds(0, 7)], s2)
    drain(got3.at[:, pl.ds(0, 7)], s3)
    drain(got4.at[:, pl.ds(0, 7)], s4)
    drain(surge.at[:, pl.ds(0, 7)], s5)
    drain(got6.at[pl.ds(0, 15)], s6)
    drain(got7.at[pl.ds(0, 7)], s7)
    drain(got8, s8)


def shards(site_ln, site_of, county_of, tract_of, comp_type, comp_qty, amplify, frag_median, frag_step, frag_beta, state_cost):
    vmem = pltpu.VMEM
    i32 = jnp.int32
    dma = pltpu.SemaphoreType.DMA
    scratch = [
        vmem((2 * HALF, LANES), F32), vmem((2, QUARTER, LANES), i32),
        vmem((2, 1, LANES), i32), vmem((2, 1, LANES), i32), vmem((2, 1, LANES), i32),
        vmem((2, GROUPS, LANES), i32), vmem((2, GROUPS, LANES), i32), vmem((2, GROUPS, LANES), F32),
        vmem((2, LANES), F32), vmem((2, LANES), F32), vmem((2, LANES), F32), vmem((3, TYPES), F32),
        vmem((2, LINE, LINE, QUARTER, LANES), i32),
    ]
    scratch += [vmem((2, GROUPS, LANES), F32)] * 7
    scratch += [
        vmem((TYPES, GROUPS * WIDE), BF16), vmem((LANES, GROUPS * WIDE), BF16),
        vmem((2 * GROUPS, HALF, LANES), F32), vmem((2 * GROUPS, HALF, LANES), F32),
        vmem((2, COUNTIES, HALF, LANES), F32), vmem((2, LINE, 2, HALF, LANES), F32),
        vmem((2, 2, HALF, LANES), F32), vmem((2, LINE, 2, HALF, LANES), F32),
        vmem((2, 16, LANES), BF16), vmem((2, LINE, 16, LANES), BF16),
        vmem((LANES, 3 * WIDE), BF16), vmem((LANES, 3 * WIDE), BF16),
        vmem((16, LINE, LANES), F32), vmem((16, LINE, LANES), F32),
        vmem((LINE, 2, LANES), F32), vmem((LINE, 2, LANES), F32),
        vmem((LINE, 1, LANES), F32), vmem((3 * LINE, 1, LANES), F32),
    ]
    scratch += [dma((6,)), dma((5,)), dma((6,)), dma((6,))]
    scratch += [dma, dma((2,)), dma, dma((2, LINE))] + [dma] * 12
    loss, avg = pl.pallas_call(
        kernel,
        out_shape=(jax.ShapeDtypeStruct((16, 16), F32), jax.ShapeDtypeStruct((1, 16), F32)),
        in_specs=[pl.BlockSpec(memory_space=pltpu.HBM)] * 11,
        out_specs=(pl.BlockSpec(memory_space=pltpu.VMEM),) * 2,
        scratch_shapes=scratch,
        compiler_params=pltpu.CompilerParams(
            collective_id=0, has_side_effects=True, vmem_limit_bytes=56 * 1024 * 1024
        ),
    )(
        site_ln, site_of.reshape(1, LANES), county_of.reshape(1, LANES), tract_of.reshape(1, LANES),
        comp_type, comp_qty, amplify,
        frag_median.reshape(2, LANES), frag_step.reshape(2, LANES), frag_beta.reshape(2, LANES), state_cost,
    )
    return loss, avg.reshape(16)


def solution(mesh):
    in_specs = (
        P("real", "bld"), P("bld"), P("bld"), P("bld"), P(None, "bld"), P(None, "bld"), P(None, "bld"),
        P(), P(), P(), P(),
    )
    out_specs = (P("bld", "real"), P("bld"))
    return jax.shard_map(shards, mesh=mesh, in_specs=in_specs, out_specs=out_specs, check_vma=False)
```

```python
import jax
import jax.numpy as jnp
from jax import lax
from jax.experimental import pallas as pl
from jax.experimental.pallas import tpu as pltpu
from jax.sharding import PartitionSpec as P

LINE = 8
GROUPS = 24
TYPES = 256
COUNTIES = 16
LANES = 128
HALF = 8
WIDE = 2 * LANES
REALS_ALL = 64.0
HALF_POINT = 385.0
ROOT_HALF = 0.7071067811865476
MESH = pl.DeviceIdType.MESH
F32 = jnp.float32
BF16 = jnp.bfloat16
HIGHEST = lax.Precision.HIGHEST
NT = (((1,), (1,)), ((), ()))
QUARTER = 4
STEPS = 65535.0 / 8.0
FAR_FIRST = (4, 3, 5, 2, 6, 1, 7)
CHUNK = 4


def lanes_of(table, index):
    return jnp.take_along_axis(table, index, axis=1, mode="promise_in_bounds")


def drain(ref, sem):
    pltpu.make_async_copy(ref, ref, sem).wait()


def kernel(
    site_ln, site_of, county_of, tract_of, comp_type, comp_qty, amplify,
    frag_median, frag_step, frag_beta, state_cost,
    loss_out, avg_out,
    b_ln, packed, b_site, b_county, b_tract, b_type, b_qty, b_amp,
    t_med, t_step, t_beta, t_cost,
    sites, p_base, p_inv, p_step, p_half, p_c0, p_c1, p_c2,
    hot, spread, args, weight,
    part, got3, half_sum, got4, surge_own, surge,
    dest, terms, tract_part, got6, rows, got7, joint, got8,
    loc_sem, par_sem, bld_send, bld_recv,
    s1, r1, s2, r2, s3, r3, s4, r4, s5, r5, s6, r6, s7, r7, s8, r8,
):
    me = lax.axis_index("bld")
    x = lax.axis_index("real")
    z = me // (2 * LINE)
    y = lax.rem(me // 2, LINE)
    c = lax.rem(me, 2)

    def at(zz, yy, cc):
        return {"bld": (zz * LINE + yy) * 2 + cc}

    def send(src, dst, ssem, rsem, who):
        pltpu.make_async_remote_copy(
            src_ref=src, dst_ref=dst, send_sem=ssem, recv_sem=rsem,
            device_id=who, device_id_type=MESH,
        ).start()

    barrier = pltpu.get_barrier_semaphore()

    def hello(who):
        pl.semaphore_signal(barrier, inc=1, device_id=who, device_id_type=MESH)

    for i in FAR_FIRST:
        for h in range(2):
            hello(at(z, lax.rem(y + i, LINE), h))
            hello(at(lax.rem(z + i, LINE), y, h))
    for i in (2, 1, 3):
        hello({"real": lax.rem(x + i, 4)})
    hello(at(z, y, 1 - c))

    buildings = (
        (site_of, b_site), (county_of, b_county), (tract_of, b_tract),
        (comp_type, b_type), (comp_qty, b_qty), (amplify, b_amp),
    )
    tables = ((frag_median, t_med), (frag_step, t_step), (frag_beta, t_beta), (state_cost, t_cost))
    own = [pltpu.make_async_copy(a, b.at[0], loc_sem.at[n]) for n, (a, b) in enumerate(buildings)]
    own += [pltpu.make_async_copy(a, b, par_sem.at[n]) for n, (a, b) in enumerate(tables)]
    own.append(pltpu.make_async_copy(site_ln, b_ln, par_sem.at[4]))
    for copy in own:
        copy.start()

    for copy in own:
        copy.wait()
    fixed = ((b_ln[...] + 4.0) * STEPS + 0.5).astype(jnp.int32)
    for h in range(2):
        first = h * HALF
        packed[h] = fixed[first : first + QUARTER] | (fixed[first + QUARTER : first + HALF] << 16)
    pl.semaphore_wait(barrier, 1 + 4 * (LINE - 1) + 3)

    p = y * (1 - c) + z * c
    q = z * (1 - c) + y * c
    mine = sites.at[c, q, p]
    local = pltpu.make_async_copy(packed.at[c], mine, r1.at[c])
    local.start()
    for i in FAR_FIRST:
        pp = lax.rem(p + i, LINE)
        for h in range(2):
            zz = q * (1 - c) + pp * c
            yy = pp * (1 - c) + q * c
            send(packed.at[h], mine, s1, r1.at[c], at(zz, yy, h))
    send(packed.at[1 - c], mine, s1, r1.at[c], at(z, y, 1 - c))
    trade = [
        pltpu.make_async_remote_copy(
            src_ref=b.at[0], dst_ref=b.at[1], send_sem=bld_send.at[n], recv_sem=bld_recv.at[n],
            device_id=at(z, y, 1 - c), device_id_type=MESH,
        )
        for n, (a, b) in enumerate(buildings)
    ]
    for copy in trade:
        copy.start()

    drain(sites.at[0, z], r1.at[0])
    for i in FAR_FIRST:
        send(sites.at[0, z], sites.at[0, z], s2, r2.at[0, i], at(lax.rem(z + i, LINE), y, c))
    drain(sites.at[1, y], r1.at[1])
    for i in FAR_FIRST:
        send(sites.at[1, y], sites.at[1, y], s2, r2.at[1, i], at(z, lax.rem(y + i, LINE), c))

    for copy in trade:
        copy.wait()
    inv_row = ROOT_HALF / t_beta[...]
    step_row = t_step[...] * inv_row
    med_row = t_med[...]
    cost = t_cost[...]

    def cost_rows(level):
        now = cost[level : level + 1]
        if level:
            now = now - cost[level - 1 : level]
        return now[:, :LANES], now[:, LANES:]

    def pair(table):
        return table[0:1], table[1:2]

    looked = (
        (pair(med_row), p_base), (pair(inv_row), p_inv), (pair(step_row), p_step),
        (cost_rows(0), p_c0), (cost_rows(1), p_c1), (cost_rows(2), p_c2),
    )
    for bh in range(2):
        for g in range(0, GROUPS, 8):
            index = b_type[bh, g : g + 8, :]
            low = index & (LANES - 1)
            high = index >= LANES
            for (first, second), into in looked:
                value = jnp.where(
                    high,
                    lanes_of(jnp.broadcast_to(second, (8, LANES)), low),
                    lanes_of(jnp.broadcast_to(first, (8, LANES)), low),
                )
                if into is p_base:
                    value = b_amp[bh, g : g + 8, :] - value
                into[bh, g : g + 8, :] = value
            p_half[bh, g : g + 8, :] = 0.5 * b_qty[bh, g : g + 8, :].astype(F32)

    one = jnp.ones((16, LANES), BF16)
    zero = jnp.zeros((16, LANES), BF16)
    count = lax.broadcasted_iota(jnp.int32, (16, LANES), 0)

    counts = [(count + 16 * n).astype(F32).astype(BF16) for n in range(TYPES // 16)]

    def make_hot(g, _):
        for bh in range(2):
            types = jnp.broadcast_to(b_type[bh, pl.ds(g, 1), :], (16, LANES)).astype(F32).astype(BF16)
            columns = pl.ds(pl.multiple_of(g * WIDE + bh * LANES, LANES), LANES)
            for n in range(TYPES // 16):
                hot[n * 16 : (n + 1) * 16, columns] = jnp.where(types == counts[n], one, zero)
        return 0

    lax.fori_loop(0, GROUPS, make_hot, 0)

    for bh in range(2):
        owner = b_tract[bh] // 16
        place = (owner & 15) * LINE + owner // 16
        place = jnp.broadcast_to(place, (16, LANES)).astype(F32).astype(BF16)
        for n in range(8):
            value = jnp.where(place == counts[n], one, zero)
            for piece in range(3):
                dest[n * 16 : (n + 1) * 16, piece * WIDE + bh * LANES : piece * WIDE + (bh + 1) * LANES] = value

    upper = (count >= HALF).astype(jnp.int32)

    def pair_masks(ref, bh):
        value = jnp.broadcast_to(ref, (16, LANES)) - upper
        value = value.astype(F32).astype(BF16)
        return [jnp.where(value == jnp.asarray(2 * n, BF16), one, zero) for n in range(8)]

    low = [jnp.broadcast_to(b_site[bh] & (LANES - 1), (HALF, LANES)) for bh in range(2)]
    high = [jnp.broadcast_to(b_site[bh] // LANES, (HALF, LANES)) for bh in range(2)]
    second = (lax.broadcasted_iota(jnp.int32, (HALF, LANES), 0) >= QUARTER).astype(jnp.int32)
    apart = [[high[bh] - second * stride for bh in range(2)] for stride in (2, 16)]
    level = [jnp.zeros((HALF, LANES), jnp.int32) for _ in range(2)]

    def pick(level, route, line):
        for n in range(0, LINE, 2):
            tile = jnp.concatenate([sites[route, line, n], sites[route, line, n + 1]], axis=0)
            block = (line * 16 + 2 * n) if route == 0 else (n * 16 + line * 2 + 1)
            level = [
                jnp.where(apart[route][bh] == block, lanes_of(tile, low[bh]), level[bh]) for bh in range(2)
            ]
        return level

    level = pick(level, 0, z)
    level = pick(level, 1, y)
    for i in (1, 7, 2, 6, 3, 5, 4):
        zz = lax.rem(z + LINE - i, LINE)
        drain(sites.at[0, zz], r2.at[0, i])
        level = pick(level, 0, zz)
        yy = lax.rem(y + LINE - i, LINE)
        drain(sites.at[1, yy], r2.at[1, i])
        level = pick(level, 1, yy)

    for bh in range(2):
        word = level[bh][:QUARTER] | level[bh][QUARTER:]
        both_halves = jnp.concatenate([word & 0xFFFF, (word >> 16) & 0xFFFF], axis=0)
        level[bh] = both_halves.astype(F32) * (1.0 / STEPS) - 4.0

    county_masks = [pair_masks(b_county[bh], bh) for bh in range(2)]
    sums = None
    for j in range(GROUPS // CHUNK + 1):
        if j < GROUPS // CHUNK:
            for g in range(j * CHUNK, (j + 1) * CHUNK):
                for bh in range(2):
                    arg = (level[bh] + p_base[bh, g : g + 1, :]) * p_inv[bh, g : g + 1, :]
                    dam = p_half[bh, g : g + 1, :] * (1.0 + lax.erf(arg))
                    args[g * 2 + bh] = arg
                    weight[g * 2 + bh] = dam * p_c0[bh, g : g + 1, :]
                    twice = jnp.concatenate([dam, dam], axis=0).astype(BF16)
                    first = g * WIDE + bh * LANES
                    for n in range(8):
                        spread[n * 16 : (n + 1) * 16, first : first + LANES] = twice * county_masks[bh][n]
        if j:
            columns = slice((j - 1) * CHUNK * WIDE, j * CHUNK * WIDE)
            found = lax.dot_general(spread[:, columns], hot[:, columns], NT, preferred_element_type=F32)
            sums = found if sums is None else sums + found

    part[0] = sums[:, :LANES].reshape(COUNTIES, HALF, LANES)
    part[1] = sums[:, LANES:].reshape(COUNTIES, HALF, LANES)

    for i in FAR_FIRST:
        yy = lax.rem(y + i, LINE)
        send(part.at[0, pl.ds(2 * yy, 2)], got3.at[0, y], s3, r3, at(z, yy, c))
        zz = lax.rem(z + i, LINE)
        send(part.at[1, pl.ds(2 * zz, 2)], got3.at[1, z], s3, r3, at(zz, y, c))
    got3[0, y] = part[0, pl.ds(2 * y, 2)]
    got3[1, z] = part[1, pl.ds(2 * z, 2)]

    def more(first, last):
        def weigh(g, _):
            row_at = pl.ds(g, 1)
            for bh in range(2):
                arg = args[g * 2 + bh]
                step = p_step[bh, row_at, :]
                rest = (1.0 + lax.erf(arg - step)) * p_c1[bh, row_at, :]
                rest = rest + (1.0 + lax.erf(arg - 2.0 * step)) * p_c2[bh, row_at, :]
                weight[g * 2 + bh] = weight[g * 2 + bh] + p_half[bh, row_at, :] * rest
            return 0

        lax.fori_loop(first, last, weigh, 0, unroll=4)

    more(0, 8)
    drain(got3.at[:, pl.ds(0, 7)], r3)

    for th in range(2):
        total = got3[th, 0]
        for n in range(1, LINE):
            total = total + got3[th, n]
        half_sum[th] = total
    for i in FAR_FIRST:
        send(half_sum.at[0], got4.at[0, z], s4, r4, at(lax.rem(z + i, LINE), y, c))
        send(half_sum.at[1], got4.at[1, y], s4, r4, at(z, lax.rem(y + i, LINE), c))
    got4[0, z] = half_sum[0]
    got4[1, y] = half_sum[1]
    more(8, 16)
    drain(got4.at[:, pl.ds(0, 7)], r4)

    for th in range(2):
        total = got4[th, 0]
        for n in range(1, LINE):
            total = total + got4[th, n]
        factor = (1.0 + total / (total + HALF_POINT)).reshape(16, LANES)
        surge_own[th] = factor.astype(BF16)
    for i in FAR_FIRST:
        send(surge_own.at[0], surge.at[0, y], s5, r5, at(z, lax.rem(y + i, LINE), c))
        send(surge_own.at[1], surge.at[1, z], s5, r5, at(lax.rem(z + i, LINE), y, c))
    surge[0, y] = surge_own[0]
    surge[1, z] = surge_own[1]
    more(16, 24)
    drain(surge.at[:, pl.ds(0, 7)], r5)

    factors = [surge[th].reshape(COUNTIES * HALF, LANES) for th in range(2)]
    both = jnp.concatenate(factors, axis=1)

    def apply(g, total):
        columns = pl.ds(pl.multiple_of(g * WIDE, WIDE), WIDE)
        found = jnp.dot(both, hot[:, columns], preferred_element_type=F32)
        tiles = jnp.concatenate([weight[g * 2], weight[g * 2 + 1]], axis=1)
        return total + found.reshape(COUNTIES, HALF, WIDE) * tiles[None]

    total = lax.fori_loop(0, GROUPS, apply, jnp.zeros((COUNTIES, HALF, WIDE), F32), unroll=8)

    for bh in range(2):
        county = jnp.broadcast_to(b_county[bh], (HALF, LANES))
        loss = jnp.zeros((HALF, LANES), F32)
        for n in range(COUNTIES):
            loss = loss + jnp.where(county == n, total[n, :, bh * LANES : (bh + 1) * LANES], 0.0)
        masks = pair_masks(b_tract[bh] & 15, bh)
        left = loss
        for piece in range(3):
            rounded = left.astype(BF16)
            left = left - rounded.astype(F32)
            twice = jnp.concatenate([rounded.astype(F32)] * 2, axis=0).astype(BF16)
            for n in range(8):
                terms[n * 16 : (n + 1) * 16, piece * WIDE + bh * LANES : piece * WIDE + (bh + 1) * LANES] = (
                    twice * masks[n]
                )

    tract_part[...] = lax.dot_general(dest[...], terms[...], NT, preferred_element_type=F32).reshape(16, LINE, LANES)

    for i in FAR_FIRST:
        yy = lax.rem(y + i, LINE)
        for h in range(2):
            send(tract_part.at[yy * 2 + h], got6.at[c * LINE + y], s6, r6, at(z, yy, h))
    send(tract_part.at[y * 2 + 1 - c], got6.at[c * LINE + y], s6, r6, at(z, y, 1 - c))
    got6[c * LINE + y] = tract_part[y * 2 + c]
    drain(got6.at[pl.ds(0, 15)], r6)

    halves = []
    for h in range(2):
        total = got6[h * LINE]
        for n in range(1, LINE):
            total = total + got6[h * LINE + n]
        halves.append(total)
        for n in range(LINE):
            rows[n, h : h + 1, :] = total[n : n + 1]
    total = halves[0] + halves[1]
    for n in range(LINE):
        joint[n] = total[n : n + 1]
    for i, k in ((4, 2), (4, 1), (4, 3), (3, 2), (5, 2), (4, 0), (3, 1), (3, 3), (5, 1), (5, 3), (2, 2), (6, 2), (3, 0), (5, 0),
                 (2, 1), (2, 3), (6, 1), (6, 3), (1, 2), (7, 2), (2, 0), (6, 0), (1, 1), (1, 3), (7, 1), (7, 3), (0, 2),
                 (1, 0), (7, 0), (0, 1), (0, 3)):
        zz = lax.rem(z + i, LINE)
        if k == 0:
            send(rows.at[zz], got7.at[z], s7, r7, at(zz, y, c))
        else:
            who = {"bld": (zz * LINE + y) * 2 + c, "real": lax.rem(x + k, 4)}
            send(joint.at[zz], got8.at[(k - 1) * LINE + z], s8, r8, who)
    got7[z] = rows[z]
    drain(got7.at[pl.ds(0, 7)], r7)
    final = got7[0]
    for n in range(1, LINE):
        final = final + got7[n]

    lane = lax.broadcasted_iota(jnp.int32, (16, LANES), 1)
    where_tract = lane // HALF == lax.broadcasted_iota(jnp.int32, (16, LANES), 0)
    from_lane = lax.broadcasted_iota(jnp.int32, (LANES, 16), 0)
    to_lane = lax.broadcasted_iota(jnp.int32, (LANES, 16), 1)
    result = jnp.zeros((16, 16), F32)
    for h in range(2):
        picked = jnp.where(where_tract, jnp.broadcast_to(final[h : h + 1], (16, LANES)), 0.0)
        put = ((from_lane & (HALF - 1)) + h * HALF == to_lane).astype(F32)
        result = result + jnp.dot(picked, put, precision=HIGHEST, preferred_element_type=F32)
    loss_out[...] = result

    drain(got8, r8)
    over = [final[0:1] + final[1:2]] + [got8[n] for n in range(3 * LINE)]
    while len(over) > 1:
        over = [sum(over[n : n + 2]) for n in range(0, len(over), 2)]
    over = jnp.broadcast_to(over[0], (HALF, LANES))
    for shift in (1, 2, 4):
        over = over + pltpu.roll(over, LANES - shift, 1)
    index = (lax.broadcasted_iota(jnp.int32, (HALF, LANES), 1) * HALF) & (LANES - 1)
    avg_out[...] = lanes_of(over, index)[0:1, 0:16] * (1.0 / REALS_ALL)

    drain(sites.at[0, pl.ds(0, 3), pl.ds(0, 5)], s1)
    drain(sites.at[:, pl.ds(0, 7)], s2)
    drain(got3.at[:, pl.ds(0, 7)], s3)
    drain(got4.at[:, pl.ds(0, 7)], s4)
    drain(surge.at[:, pl.ds(0, 7)], s5)
    drain(got6.at[pl.ds(0, 15)], s6)
    drain(got7.at[pl.ds(0, 7)], s7)
    drain(got8, s8)


def shards(site_ln, site_of, county_of, tract_of, comp_type, comp_qty, amplify, frag_median, frag_step, frag_beta, state_cost):
    vmem = pltpu.VMEM
    i32 = jnp.int32
    dma = pltpu.SemaphoreType.DMA
    scratch = [
        vmem((2 * HALF, LANES), F32), vmem((2, QUARTER, LANES), i32),
        vmem((2, 1, LANES), i32), vmem((2, 1, LANES), i32), vmem((2, 1, LANES), i32),
        vmem((2, GROUPS, LANES), i32), vmem((2, GROUPS, LANES), i32), vmem((2, GROUPS, LANES), F32),
        vmem((2, LANES), F32), vmem((2, LANES), F32), vmem((2, LANES), F32), vmem((3, TYPES), F32),
        vmem((2, LINE, LINE, QUARTER, LANES), i32),
    ]
    scratch += [vmem((2, GROUPS, LANES), F32)] * 7
    scratch += [
        vmem((TYPES, GROUPS * WIDE), BF16), vmem((LANES, GROUPS * WIDE), BF16),
        vmem((2 * GROUPS, HALF, LANES), F32), vmem((2 * GROUPS, HALF, LANES), F32),
        vmem((2, COUNTIES, HALF, LANES), F32), vmem((2, LINE, 2, HALF, LANES), F32),
        vmem((2, 2, HALF, LANES), F32), vmem((2, LINE, 2, HALF, LANES), F32),
        vmem((2, 16, LANES), BF16), vmem((2, LINE, 16, LANES), BF16),
        vmem((LANES, 3 * WIDE), BF16), vmem((LANES, 3 * WIDE), BF16),
        vmem((16, LINE, LANES), F32), vmem((16, LINE, LANES), F32),
        vmem((LINE, 2, LANES), F32), vmem((LINE, 2, LANES), F32),
        vmem((LINE, 1, LANES), F32), vmem((3 * LINE, 1, LANES), F32),
    ]
    scratch += [dma((6,)), dma((5,)), dma((6,)), dma((6,))]
    scratch += [dma, dma((2,)), dma, dma((2, LINE))] + [dma] * 12
    loss, avg = pl.pallas_call(
        kernel,
        out_shape=(pltpu.VMEM((16, 16), F32), pltpu.VMEM((1, 16), F32)),
        in_specs=[pl.BlockSpec(memory_space=pltpu.HBM)] * 11,
        out_specs=(pl.BlockSpec(memory_space=pltpu.VMEM),) * 2,
        scratch_shapes=scratch,
        compiler_params=pltpu.CompilerParams(
            collective_id=0, has_side_effects=True, vmem_limit_bytes=56 * 1024 * 1024
        ),
    )(
        site_ln, site_of.reshape(1, LANES), county_of.reshape(1, LANES), tract_of.reshape(1, LANES),
        comp_type, comp_qty, amplify,
        frag_median.reshape(2, LANES), frag_step.reshape(2, LANES), frag_beta.reshape(2, LANES), state_cost,
    )
    return loss, avg.reshape(16)


def solution(mesh):
    in_specs = (
        P("real", "bld"), P("bld"), P("bld"), P("bld"), P(None, "bld"), P(None, "bld"), P(None, "bld"),
        P(), P(), P(), P(),
    )
    out_specs = (P("bld", "real"), P("bld"))
    return jax.shard_map(shards, mesh=mesh, in_specs=in_specs, out_specs=out_specs, check_vma=False)
```

```python
import jax
import jax.numpy as jnp
from jax import lax
from jax.experimental import pallas as pl
from jax.experimental.pallas import tpu as pltpu
from jax.sharding import PartitionSpec as P

LINE = 8
GROUPS = 24
TYPES = 256
COUNTIES = 16
LANES = 128
HALF = 8
WIDE = 2 * LANES
REALS_ALL = 64.0
HALF_POINT = 385.0
ROOT_HALF = 0.7071067811865476
MESH = pl.DeviceIdType.MESH
F32 = jnp.float32
BF16 = jnp.bfloat16
HIGHEST = lax.Precision.HIGHEST
NT = (((1,), (1,)), ((), ()))
QUARTER = 4
STEPS = 65535.0 / 8.0
FAR_FIRST = (4, 3, 5, 2, 6, 1, 7)
CHUNK = 4


def lanes_of(table, index):
    return jnp.take_along_axis(table, index, axis=1, mode="promise_in_bounds")


def drain(ref, sem):
    pltpu.make_async_copy(ref, ref, sem).wait()


def kernel(
    site_ln, site_of, county_of, tract_of, comp_type, comp_qty, amplify,
    frag_median, frag_step, frag_beta, state_cost,
    loss_out, avg_out,
    b_ln, packed, b_site, b_county, b_tract, b_type, b_qty, b_amp,
    t_med, t_step, t_beta, t_cost,
    line, spare, sites, p_base, p_inv, p_step, p_half, p_c0, p_c1, p_c2,
    hot, hot_t, spread, args, weight,
    part, got3, half_sum, got4, surge_own, surge,
    dest, terms, tract_part, got6, rows, got7, joint, got8,
    loc_sem, par_sem, bld_send, bld_recv,
    s1, r1, s2, r2, s3, r3, s4, r4, s5, r5, s6, r6, s7, r7, s8, r8,
):
    me = lax.axis_index("bld")
    x = lax.axis_index("real")
    z = me // (2 * LINE)
    y = lax.rem(me // 2, LINE)
    c = lax.rem(me, 2)

    def at(zz, yy, cc):
        return {"bld": (zz * LINE + yy) * 2 + cc}

    def send(src, dst, ssem, rsem, who):
        pltpu.make_async_remote_copy(
            src_ref=src, dst_ref=dst, send_sem=ssem, recv_sem=rsem,
            device_id=who, device_id_type=MESH,
        ).start()

    barrier = pltpu.get_barrier_semaphore()

    def hello(who):
        pl.semaphore_signal(barrier, inc=1, device_id=who, device_id_type=MESH)

    for i in FAR_FIRST:
        for h in range(2):
            hello(at(z, lax.rem(y + i, LINE), h))
            hello(at(lax.rem(z + i, LINE), y, h))
    for i in (2, 1, 3):
        hello({"real": lax.rem(x + i, 4)})
    hello(at(z, y, 1 - c))

    buildings = (
        (site_of, b_site), (county_of, b_county), (tract_of, b_tract),
        (comp_type, b_type), (comp_qty, b_qty), (amplify, b_amp),
    )
    tables = ((frag_median, t_med), (frag_step, t_step), (frag_beta, t_beta), (state_cost, t_cost))
    own = [pltpu.make_async_copy(a, b.at[0], loc_sem.at[n]) for n, (a, b) in enumerate(buildings)]
    own += [pltpu.make_async_copy(a, b, par_sem.at[n]) for n, (a, b) in enumerate(tables)]
    own.append(pltpu.make_async_copy(site_ln, b_ln, par_sem.at[4]))
    for copy in own:
        copy.start()

    for copy in own:
        copy.wait()
    fixed = ((b_ln[...] + 4.0) * STEPS + 0.5).astype(jnp.int32)
    for h in range(2):
        first = h * HALF
        packed[h] = fixed[first : first + QUARTER] | (fixed[first + QUARTER : first + HALF] << 16)
    pl.semaphore_wait(barrier, 1 + 4 * (LINE - 1) + 3)

    p = y * (1 - c) + z * c
    q = z * (1 - c) + y * c
    mine = line.at[c, p]
    local = pltpu.make_async_copy(packed.at[c], mine, r1.at[c])
    local.start()
    for i in FAR_FIRST:
        pp = lax.rem(p + i, LINE)
        for h in range(2):
            zz = q * (1 - c) + pp * c
            yy = pp * (1 - c) + q * c
            send(packed.at[h], mine, s1, r1.at[c], at(zz, yy, h))
    send(packed.at[1 - c], mine, s1, r1.at[c], at(z, y, 1 - c))
    trade = [
        pltpu.make_async_remote_copy(
            src_ref=b.at[0], dst_ref=b.at[1], send_sem=bld_send.at[n], recv_sem=bld_recv.at[n],
            device_id=at(z, y, 1 - c), device_id_type=MESH,
        )
        for n, (a, b) in enumerate(buildings)
    ]
    for copy in trade:
        copy.start()

    def pairs(route, own_line):
        drain(line.at[route], r1.at[route])
        for n in range(LINE // 2):
            sites[route, own_line, n] = jnp.concatenate([line[route, 2 * n], line[route, 2 * n + 1]], axis=0)

    pairs(0, z)
    for i in FAR_FIRST:
        send(sites.at[0, z], sites.at[0, z], s2, r2.at[0, i], at(lax.rem(z + i, LINE), y, c))
    pairs(1, y)
    for i in FAR_FIRST:
        send(sites.at[1, y], sites.at[1, y], s2, r2.at[1, i], at(z, lax.rem(y + i, LINE), c))

    for copy in trade:
        copy.wait()
    inv_row = ROOT_HALF / t_beta[...]
    step_row = t_step[...] * inv_row
    med_row = t_med[...]
    cost = t_cost[...]

    def cost_rows(level):
        now = cost[level : level + 1]
        if level:
            now = now - cost[level - 1 : level]
        return now[:, :LANES], now[:, LANES:]

    def pair(table):
        return table[0:1], table[1:2]

    looked = (
        (pair(med_row), p_base), (pair(inv_row), p_inv), (pair(step_row), p_step),
        (cost_rows(0), p_c0), (cost_rows(1), p_c1), (cost_rows(2), p_c2),
    )
    for bh in range(2):
        for g in range(0, GROUPS, 8):
            index = b_type[bh, g : g + 8, :]
            low = index & (LANES - 1)
            high = index >= LANES
            for (first, second), into in looked:
                value = jnp.where(
                    high,
                    lanes_of(jnp.broadcast_to(second, (8, LANES)), low),
                    lanes_of(jnp.broadcast_to(first, (8, LANES)), low),
                )
                if into is p_base:
                    value = b_amp[bh, g : g + 8, :] - value
                into[bh, g : g + 8, :] = value
            p_half[bh, g : g + 8, :] = 0.5 * b_qty[bh, g : g + 8, :].astype(F32)

    one = jnp.ones((16, LANES), BF16)
    zero = jnp.zeros((16, LANES), BF16)
    count = lax.broadcasted_iota(jnp.int32, (16, LANES), 0)

    counts = [(count + 16 * n).astype(F32).astype(BF16) for n in range(TYPES // 16)]

    def make_hot(g, _):
        for bh in range(2):
            types = jnp.broadcast_to(b_type[bh, pl.ds(g, 1), :], (16, LANES)).astype(F32).astype(BF16)
            columns = pl.ds(pl.multiple_of(g * WIDE + bh * LANES, LANES), LANES)
            for n in range(TYPES // 16):
                hot[n * 16 : (n + 1) * 16, columns] = jnp.where(types == counts[n], one, zero)
        columns = pl.ds(pl.multiple_of(g * WIDE, WIDE), WIDE)
        hot_t[columns, :] = hot[:, columns].T
        return 0

    lax.fori_loop(0, GROUPS, make_hot, 0)

    for bh in range(2):
        owner = b_tract[bh] // 16
        place = (owner & 15) * LINE + owner // 16
        place = jnp.broadcast_to(place, (16, LANES)).astype(F32).astype(BF16)
        for n in range(8):
            value = jnp.where(place == counts[n], one, zero)
            for piece in range(3):
                dest[n * 16 : (n + 1) * 16, piece * WIDE + bh * LANES : piece * WIDE + (bh + 1) * LANES] = value

    upper = (count >= HALF).astype(jnp.int32)

    def pair_masks(ref, bh):
        value = jnp.broadcast_to(ref, (16, LANES)) - upper
        value = value.astype(F32).astype(BF16)
        return [jnp.where(value == jnp.asarray(2 * n, BF16), one, zero) for n in range(8)]

    low = [jnp.broadcast_to(b_site[bh] & (LANES - 1), (HALF, LANES)) for bh in range(2)]
    high = [jnp.broadcast_to(b_site[bh] // LANES, (HALF, LANES)) for bh in range(2)]
    second = (lax.broadcasted_iota(jnp.int32, (HALF, LANES), 0) >= QUARTER).astype(jnp.int32)
    apart = [[high[bh] - second * stride for bh in range(2)] for stride in (2, 16)]
    level = [jnp.zeros((HALF, LANES), jnp.int32) for _ in range(2)]

    def pick(level, route, other):
        for n in range(0, LINE, 2):
            tile = sites[route, other, n // 2]
            block = (other * 16 + 2 * n) if route == 0 else (n * 16 + other * 2 + 1)
            level = [
                jnp.where(apart[route][bh] == block, lanes_of(tile, low[bh]), level[bh]) for bh in range(2)
            ]
        return level

    level = pick(level, 0, z)
    level = pick(level, 1, y)
    for i in (1, 7, 2, 6, 3, 5, 4):
        zz = lax.rem(z + LINE - i, LINE)
        drain(sites.at[0, zz], r2.at[0, i])
        level = pick(level, 0, zz)
        yy = lax.rem(y + LINE - i, LINE)
        drain(sites.at[1, yy], r2.at[1, i])
        level = pick(level, 1, yy)

    for bh in range(2):
        word = level[bh][:QUARTER] | level[bh][QUARTER:]
        both_halves = jnp.concatenate([word & 0xFFFF, (word >> 16) & 0xFFFF], axis=0)
        level[bh] = both_halves.astype(F32) * (1.0 / STEPS) - 4.0

    county_masks = [pair_masks(b_county[bh], bh) for bh in range(2)]
    sums = None
    for j in range(GROUPS // CHUNK + 1):
        if j < GROUPS // CHUNK:
            for g in range(j * CHUNK, (j + 1) * CHUNK):
                for bh in range(2):
                    arg = (level[bh] + p_base[bh, g : g + 1, :]) * p_inv[bh, g : g + 1, :]
                    dam = p_half[bh, g : g + 1, :] * (1.0 + lax.erf(arg))
                    args[g * 2 + bh] = arg
                    weight[g * 2 + bh] = dam * p_c0[bh, g : g + 1, :]
                    twice = jnp.concatenate([dam, dam], axis=0).astype(BF16)
                    first = g * WIDE + bh * LANES
                    for n in range(8):
                        spread[n * 16 : (n + 1) * 16, first : first + LANES] = twice * county_masks[bh][n]
        if j:
            columns = slice((j - 1) * CHUNK * WIDE, j * CHUNK * WIDE)
            found = jnp.dot(spread[:, columns], hot_t[columns, :], preferred_element_type=F32)
            sums = found if sums is None else sums + found

    part[0] = sums[:, :LANES].reshape(COUNTIES, HALF, LANES)
    part[1] = sums[:, LANES:].reshape(COUNTIES, HALF, LANES)

    for i in FAR_FIRST:
        yy = lax.rem(y + i, LINE)
        send(part.at[0, pl.ds(2 * yy, 2)], got3.at[0, y], s3, r3, at(z, yy, c))
        zz = lax.rem(z + i, LINE)
        send(part.at[1, pl.ds(2 * zz, 2)], got3.at[1, z], s3, r3, at(zz, y, c))
    got3[0, y] = part[0, pl.ds(2 * y, 2)]
    got3[1, z] = part[1, pl.ds(2 * z, 2)]

    def more(first, last):
        def weigh(g, _):
            row_at = pl.ds(g, 1)
            for bh in range(2):
                arg = args[g * 2 + bh]
                step = p_step[bh, row_at, :]
                rest = (1.0 + lax.erf(arg - step)) * p_c1[bh, row_at, :]
                rest = rest + (1.0 + lax.erf(arg - 2.0 * step)) * p_c2[bh, row_at, :]
                weight[g * 2 + bh] = weight[g * 2 + bh] + p_half[bh, row_at, :] * rest
            return 0

        lax.fori_loop(first, last, weigh, 0, unroll=4)

    more(0, 8)
    drain(got3.at[:, pl.ds(0, 7)], r3)

    for th in range(2):
        total = got3[th, 0]
        for n in range(1, LINE):
            total = total + got3[th, n]
        half_sum[th] = total
    for i in FAR_FIRST:
        send(half_sum.at[0], got4.at[0, z], s4, r4, at(lax.rem(z + i, LINE), y, c))
        send(half_sum.at[1], got4.at[1, y], s4, r4, at(z, lax.rem(y + i, LINE), c))
    got4[0, z] = half_sum[0]
    got4[1, y] = half_sum[1]
    more(8, 16)
    drain(got4.at[:, pl.ds(0, 7)], r4)

    for th in range(2):
        total = got4[th, 0]
        for n in range(1, LINE):
            total = total + got4[th, n]
        factor = (1.0 + total / (total + HALF_POINT)).reshape(16, LANES)
        surge_own[th] = factor.astype(BF16)
    for i in FAR_FIRST:
        send(surge_own.at[0], surge.at[0, y], s5, r5, at(z, lax.rem(y + i, LINE), c))
        send(surge_own.at[1], surge.at[1, z], s5, r5, at(lax.rem(z + i, LINE), y, c))
    surge[0, y] = surge_own[0]
    surge[1, z] = surge_own[1]
    more(16, 24)
    drain(surge.at[:, pl.ds(0, 7)], r5)

    factors = [surge[th].reshape(COUNTIES * HALF, LANES) for th in range(2)]
    both = jnp.concatenate(factors, axis=1)

    def apply(g, total):
        columns = pl.ds(pl.multiple_of(g * WIDE, WIDE), WIDE)
        found = jnp.dot(both, hot[:, columns], preferred_element_type=F32)
        tiles = jnp.concatenate([weight[g * 2], weight[g * 2 + 1]], axis=1)
        return total + found.reshape(COUNTIES, HALF, WIDE) * tiles[None]

    total = lax.fori_loop(0, GROUPS, apply, jnp.zeros((COUNTIES, HALF, WIDE), F32), unroll=8)

    for bh in range(2):
        county = jnp.broadcast_to(b_county[bh], (HALF, LANES))
        loss = jnp.zeros((HALF, LANES), F32)
        for n in range(COUNTIES):
            loss = loss + jnp.where(county == n, total[n, :, bh * LANES : (bh + 1) * LANES], 0.0)
        masks = pair_masks(b_tract[bh] & 15, bh)
        left = loss
        for piece in range(3):
            rounded = left.astype(BF16)
            left = left - rounded.astype(F32)
            twice = jnp.concatenate([rounded.astype(F32)] * 2, axis=0).astype(BF16)
            for n in range(8):
                terms[n * 16 : (n + 1) * 16, piece * WIDE + bh * LANES : piece * WIDE + (bh + 1) * LANES] = (
                    twice * masks[n]
                )

    tract_part[...] = lax.dot_general(dest[...], terms[...], NT, preferred_element_type=F32).reshape(16, LINE, LANES)

    for i in FAR_FIRST:
        yy = lax.rem(y + i, LINE)
        for h in range(2):
            send(tract_part.at[yy * 2 + h], got6.at[c * LINE + y], s6, r6, at(z, yy, h))
    send(tract_part.at[y * 2 + 1 - c], got6.at[c * LINE + y], s6, r6, at(z, y, 1 - c))
    got6[c * LINE + y] = tract_part[y * 2 + c]
    drain(got6.at[pl.ds(0, 15)], r6)

    halves = []
    for h in range(2):
        total = got6[h * LINE]
        for n in range(1, LINE):
            total = total + got6[h * LINE + n]
        halves.append(total)
        for n in range(LINE):
            rows[n, h : h + 1, :] = total[n : n + 1]
    total = halves[0] + halves[1]
    for n in range(LINE):
        joint[n] = total[n : n + 1]
    for i, k in ((4, 2), (4, 1), (4, 3), (3, 2), (5, 2), (4, 0), (3, 1), (3, 3), (5, 1), (5, 3), (2, 2), (6, 2), (3, 0), (5, 0),
                 (2, 1), (2, 3), (6, 1), (6, 3), (1, 2), (7, 2), (2, 0), (6, 0), (1, 1), (1, 3), (7, 1), (7, 3), (0, 2),
                 (1, 0), (7, 0), (0, 1), (0, 3)):
        zz = lax.rem(z + i, LINE)
        if k == 0:
            send(rows.at[zz], got7.at[z], s7, r7, at(zz, y, c))
        else:
            who = {"bld": (zz * LINE + y) * 2 + c, "real": lax.rem(x + k, 4)}
            send(joint.at[zz], got8.at[(k - 1) * LINE + z], s8, r8, who)
    got7[z] = rows[z]
    drain(got7.at[pl.ds(0, 7)], r7)
    final = got7[0]
    for n in range(1, LINE):
        final = final + got7[n]

    lane = lax.broadcasted_iota(jnp.int32, (16, LANES), 1)
    where_tract = lane // HALF == lax.broadcasted_iota(jnp.int32, (16, LANES), 0)
    from_lane = lax.broadcasted_iota(jnp.int32, (LANES, 16), 0)
    to_lane = lax.broadcasted_iota(jnp.int32, (LANES, 16), 1)
    result = jnp.zeros((16, 16), F32)
    for h in range(2):
        picked = jnp.where(where_tract, jnp.broadcast_to(final[h : h + 1], (16, LANES)), 0.0)
        put = ((from_lane & (HALF - 1)) + h * HALF == to_lane).astype(F32)
        result = result + jnp.dot(picked, put, precision=HIGHEST, preferred_element_type=F32)
    loss_out[...] = result

    drain(got8, r8)
    over = [final[0:1] + final[1:2]] + [got8[n] for n in range(3 * LINE)]
    while len(over) > 1:
        over = [sum(over[n : n + 2]) for n in range(0, len(over), 2)]
    over = jnp.broadcast_to(over[0], (HALF, LANES))
    for shift in (1, 2, 4):
        over = over + pltpu.roll(over, LANES - shift, 1)
    index = (lax.broadcasted_iota(jnp.int32, (HALF, LANES), 1) * HALF) & (LANES - 1)
    avg_out[...] = lanes_of(over, index)[0:1, 0:16] * (1.0 / REALS_ALL)

    drain(spare, s1)
    drain(sites.at[:, pl.ds(0, 7)], s2)
    drain(got3.at[:, pl.ds(0, 7)], s3)
    drain(got4.at[:, pl.ds(0, 7)], s4)
    drain(surge.at[:, pl.ds(0, 7)], s5)
    drain(got6.at[pl.ds(0, 15)], s6)
    drain(got7.at[pl.ds(0, 7)], s7)
    drain(got8, s8)


def shards(site_ln, site_of, county_of, tract_of, comp_type, comp_qty, amplify, frag_median, frag_step, frag_beta, state_cost):
    vmem = pltpu.VMEM
    i32 = jnp.int32
    dma = pltpu.SemaphoreType.DMA
    scratch = [
        vmem((2 * HALF, LANES), F32), vmem((2, QUARTER, LANES), i32),
        vmem((2, 1, LANES), i32), vmem((2, 1, LANES), i32), vmem((2, 1, LANES), i32),
        vmem((2, GROUPS, LANES), i32), vmem((2, GROUPS, LANES), i32), vmem((2, GROUPS, LANES), F32),
        vmem((2, LANES), F32), vmem((2, LANES), F32), vmem((2, LANES), F32), vmem((3, TYPES), F32),
        vmem((2, LINE, QUARTER, LANES), i32), vmem((15, QUARTER, LANES), i32), vmem((2, LINE, LINE // 2, HALF, LANES), i32),
    ]
    scratch += [vmem((2, GROUPS, LANES), F32)] * 7
    scratch += [
        vmem((TYPES, GROUPS * WIDE), BF16), vmem((GROUPS * WIDE, TYPES), BF16), vmem((LANES, GROUPS * WIDE), BF16),
        vmem((2 * GROUPS, HALF, LANES), F32), vmem((2 * GROUPS, HALF, LANES), F32),
        vmem((2, COUNTIES, HALF, LANES), F32), vmem((2, LINE, 2, HALF, LANES), F32),
        vmem((2, 2, HALF, LANES), F32), vmem((2, LINE, 2, HALF, LANES), F32),
        vmem((2, 16, LANES), BF16), vmem((2, LINE, 16, LANES), BF16),
        vmem((LANES, 3 * WIDE), BF16), vmem((LANES, 3 * WIDE), BF16),
        vmem((16, LINE, LANES), F32), vmem((16, LINE, LANES), F32),
        vmem((LINE, 2, LANES), F32), vmem((LINE, 2, LANES), F32),
        vmem((LINE, 1, LANES), F32), vmem((3 * LINE, 1, LANES), F32),
    ]
    scratch += [dma((6,)), dma((5,)), dma((6,)), dma((6,))]
    scratch += [dma, dma((2,)), dma, dma((2, LINE))] + [dma] * 12
    loss, avg = pl.pallas_call(
        kernel,
        out_shape=(pltpu.VMEM((16, 16), F32), pltpu.VMEM((1, 16), F32)),
        in_specs=[pl.BlockSpec(memory_space=pltpu.HBM)] * 11,
        out_specs=(pl.BlockSpec(memory_space=pltpu.VMEM),) * 2,
        scratch_shapes=scratch,
        compiler_params=pltpu.CompilerParams(
            collective_id=0, has_side_effects=True, vmem_limit_bytes=56 * 1024 * 1024
        ),
    )(
        site_ln, site_of.reshape(1, LANES), county_of.reshape(1, LANES), tract_of.reshape(1, LANES),
        comp_type, comp_qty, amplify,
        frag_median.reshape(2, LANES), frag_step.reshape(2, LANES), frag_beta.reshape(2, LANES), state_cost,
    )
    return loss, avg.reshape(16)


def solution(mesh):
    in_specs = (
        P("real", "bld"), P("bld"), P("bld"), P("bld"), P(None, "bld"), P(None, "bld"), P(None, "bld"),
        P(), P(), P(), P(),
    )
    out_specs = (P("bld", "real"), P("bld"))
    return jax.shard_map(shards, mesh=mesh, in_specs=in_specs, out_specs=out_specs, check_vma=False)
```
